512 devices in a mesh: row: 16 (over z_lo, core), col: 32 (over z_hi, y, x).
Axes of the slice: x: 4, y: 4, z: 16 (z_hi: 2, z_lo: 8; z = z_hi * 8 + z_lo), core: 2. Of those that a mesh axis runs over, the one named last changes fastest.
Arguments:
- inverse_anc: bfloat16 [2, 16384, 16384], P(None, 'row', 'col'), may hold values from -6 to 6
- lower_panel: bfloat16 [2, 8, 16, 256, 256], P(None, None, 'row', 'col'), may hold values from -0.125 to 0.125
- diag_inverse: float32 [2, 8, 256, 256], P(None, None, 'row'), may hold values from -6 to 6
- structure: int32 [8, 16], replicated, may hold values from 0 to 63, as said below
Outputs:
- upper_inverse: bfloat16 [2, 8, 256, 16384], P(None, None, 'row', 'col')
- diag_block: float32 [2, 8, 256, 256], P(None, None, 'row')
The draws below stay inside these ranges and needn't reach their ends.
Inputs may be any that keep to these rules, and one draw needn't show every extreme that they name: Entry r of a supernode's structure is a block from r * 4 to (r + 1) * 4 - 1.
All inputs are finite; a program needn't handle non-finite values.
Results may differ from the reference program's by a relative error of at most 0.0028.
Values may be sent and summed in bfloat16 or wider, within the bound.
No kernel may reach another device: no remote copies, remote signals or barrier semaphores. Data moves between devices by JAX's collectives and lax.ppermute only.
A program may use at most 64 MiB of HBM per device.

```python
import jax
import jax.numpy as jnp
from jax import lax

BLOCK = 256
SUPERNODES = 8
ANC_COL = 2
ANCESTORS = 64
STRUCT = 16


def draw_structure(key, part):
    key = jax.random.fold_in(key, 11)
    band = ANCESTORS // STRUCT
    offset = jax.random.randint(key, (SUPERNODES, STRUCT), 0, band, dtype=jnp.int32)
    offset = offset.at[0, 0].set(ANC_COL).at[0, STRUCT - 1].set(band - 1)
    offset = offset.at[SUPERNODES - 1, 0].set(0)
    return (offset + band * jnp.arange(STRUCT, dtype=jnp.int32)[None, :]).astype(jnp.int32)


def strengthened(result, own_key, source, target, parts, factor):
    owner, partner = [(jnp.arange(result.shape[axis_at]) // (result.shape[axis_at] // parts)).reshape([-1 if axis == axis_at else 1 for axis in range(result.ndim)]) for axis_at in (source, target)]
    chosen = jax.random.permutation(own_key, parts)[partner]
    strong = (owner == chosen) | (owner == (partner + parts // 2) % parts)
    return jnp.where(strong, factor * result, result)


def block_scale(own_key, dims, pieces, least, largest):
    gain = 1.0
    for axis_at, blocks in pieces:
        draws = jax.random.uniform(jax.random.fold_in(jax.random.fold_in(own_key, 6), axis_at), (blocks,), jnp.float32, least / len(pieces), largest / len(pieces))
        gain = gain * jnp.repeat(jnp.exp(draws), dims[axis_at] // blocks).reshape((-1,) + (1,) * (len(dims) - 1 - axis_at))
    return gain


def noise(stream_key, shape, spread, reach, pieces=(), kind=jnp.bfloat16):
    loudness = block_scale(stream_key, shape, pieces, -0.22, 0.18) if pieces else 1.0
    values = jax.random.normal(stream_key, shape, jnp.float32) * spread * loudness
    return jnp.minimum(jnp.maximum(values, -reach), reach).astype(kind)


def heavy_noise(own_key, dims, deviation, bound, cuts, heavy, held_as=jnp.bfloat16):
    entries = deviation * jax.random.normal(own_key, dims, jnp.float32)
    if cuts:
        entries = entries * block_scale(own_key, dims, cuts, -0.22, 0.18)
    return jnp.clip(strengthened(entries, jax.random.fold_in(own_key, 3), *heavy), -bound, bound).astype(held_as)


def setup_inputs(seed: int = 0) -> dict:
    splits = jax.random.split(jax.random.key(seed), 5)
    inverse_anc = noise(splits[0], (2, ANCESTORS * BLOCK, ANCESTORS * BLOCK), 1.0, 6.0, ((1, 16), (2, 32)))
    lower_panel = heavy_noise(splits[1], (2, SUPERNODES, STRUCT, BLOCK, BLOCK), (STRUCT * BLOCK) ** -0.5, 0.125, ((2, 16), (3, 32)), (2, 4, 16, 2.0))
    diag_inverse = noise(splits[2], (2, SUPERNODES, BLOCK, BLOCK), 1.0, 6.0, ((2, 16),), jnp.float32)
    structure = draw_structure(jax.random.fold_in(splits[4], 71), 0)
    return dict(inverse_anc=inverse_anc, lower_panel=lower_panel, diag_inverse=diag_inverse, structure=structure)


def one_supernode(args):
    panel, slots, dinv, table = args
    rows = jnp.take(table, slots, axis=1)
    sub = jnp.take(rows, slots, axis=3)
    lreal = panel[0].astype(jnp.float32)
    limag = panel[1].astype(jnp.float32)
    greal = sub[0].astype(jnp.float32)
    gimag = sub[1].astype(jnp.float32)
    form = 'rba,rbqc->rqac'
    real = jnp.einsum(form, lreal, greal) - jnp.einsum(form, limag, gimag)
    imag = jnp.einsum(form, lreal, gimag) + jnp.einsum(form, limag, greal)
    ureal = (-jnp.sum(real, axis=0)).astype(jnp.bfloat16)
    uimag = (-jnp.sum(imag, axis=0)).astype(jnp.bfloat16)
    ur = ureal.astype(jnp.float32)
    ui = uimag.astype(jnp.float32)
    dform = 'qac,qcd->ad'
    dreal = dinv[0] - (jnp.einsum(dform, ur, lreal) - jnp.einsum(dform, ui, limag))
    dimag = dinv[1] - (jnp.einsum(dform, ur, limag) + jnp.einsum(dform, ui, lreal))
    blocks = jnp.stack([ureal, uimag]).transpose(0, 2, 1, 3)
    full = jnp.zeros((2, BLOCK, ANCESTORS, BLOCK), blocks.dtype)
    full = full.at[:, :, slots, :].set(blocks)
    return full, jnp.stack([dreal, dimag])


def reference(inverse_anc, lower_panel, diag_inverse, structure):
    table = inverse_anc.reshape(2, ANCESTORS, BLOCK, ANCESTORS, BLOCK)
    panels = lower_panel.transpose(1, 0, 2, 3, 4)
    dinvs = diag_inverse.transpose(1, 0, 2, 3)

    def step(args):
        return one_supernode((args[0], args[1], args[2], table))

    uppers, diags = lax.map(step, (panels, structure, dinvs))
    upper_inverse = uppers.transpose(1, 0, 2, 3, 4).reshape(2, SUPERNODES, BLOCK, ANCESTORS * BLOCK)
    diag_block = diags.transpose(1, 0, 2, 3)
    return upper_inverse, diag_block
```

```python
import functools

import jax
import jax.numpy as jnp
from jax import lax
from jax.experimental import pallas as pl
from jax.experimental.pallas import tpu as pltpu
from jax.sharding import Mesh, PartitionSpec as P

BF = jnp.bfloat16
F32 = jnp.float32
ROW = ("za", "zb", "zc", "core")
COL = ("zh", "y", "xa", "h")
PLANE = ("y", "xa", "h")
VMEM_LIMIT = 48 * 1024 * 1024


def params():
    return pltpu.CompilerParams(vmem_limit_bytes=VMEM_LIMIT)


def whole(count):
    return [pl.BlockSpec(memory_space=pltpu.VMEM)] * count


def block_row(k, st, ids):
    return st[k, ids[0]] - 4 * ids[0]


def block_col(k, st, ids):
    return lax.rem(st[k, ids[1] // 2], 2)


def present(k, st, ids):
    return st[k, ids[1] // 2] // 2 == ids[1]


def pick_kernel(st, ids, block, out):
    out[:, 0] = block[...]


def pick_far_half(inverse_anc, structure, ids):
    def at(k, st, ids):
        half = 1 - lax.rem(ids[1], 2)
        return (0, block_row(k, st, ids), 2 * block_col(k, st, ids) + half)

    return pl.pallas_call(
        pick_kernel,
        grid_spec=pltpu.PrefetchScalarGridSpec(
            num_scalar_prefetch=2,
            grid=(8,),
            in_specs=[pl.BlockSpec((2, 256, 128), at)],
            out_specs=pl.BlockSpec((2, 1, 256, 128), lambda k, st, ids: (0, k, 0, 0)),
        ),
        out_shape=jax.ShapeDtypeStruct((2, 8, 256, 128), BF),
        compiler_params=params(),
    )(structure, ids, inverse_anc)


def merge_kernel(st, ids, block, got, out):
    k = pl.program_id(0)
    mine = present(k, st, ids)

    @pl.when(mine)
    def _():
        out[:, 0] = block[...]

    @pl.when(jnp.logical_not(mine))
    def _():
        out[...] = got[...]


def merge_halves(inverse_anc, got, structure, ids):
    def at(k, st, ids):
        half = lax.rem(ids[1], 2)
        return (0, block_row(k, st, ids), 2 * block_col(k, st, ids) + half)

    slab = pl.BlockSpec((2, 1, 256, 128), lambda k, st, ids: (0, k, 0, 0))
    return pl.pallas_call(
        merge_kernel,
        grid_spec=pltpu.PrefetchScalarGridSpec(
            num_scalar_prefetch=2,
            grid=(8,),
            in_specs=[pl.BlockSpec((2, 256, 128), at), slab],
            out_specs=slab,
        ),
        out_shape=jax.ShapeDtypeStruct((2, 8, 256, 128), BF),
        compiler_params=params(),
    )(structure, ids, inverse_anc, got)


def lanes_kernel(panel, out):
    x = panel[...].astype(F32).reshape(128, 256).astype(BF)
    src = lax.broadcasted_iota(jnp.int32, (256, 256), 0)
    dst = lax.broadcasted_iota(jnp.int32, (256, 256), 1)
    t = src % 16
    core = (src // 16) % 2
    zc = (src // 32) % 2
    zab = src // 64
    place = core * 128 + zc * 64 + zab * 16 + t
    perm = jnp.where(place == dst, 1.0, 0.0).astype(BF)
    y = jnp.dot(x, perm, preferred_element_type=F32)
    for c in range(2):
        half = y[:, 128 * c : 128 * c + 128].reshape(2, 8, 8, 128).astype(BF)
        for z in range(2):
            out[c, z] = half


def split_lanes(panel):
    return pl.pallas_call(
        lanes_kernel,
        in_specs=whole(1),
        out_specs=whole(1)[0],
        out_shape=jax.ShapeDtypeStruct((2, 2, 2, 8, 8, 128), BF),
        compiler_params=params(),
    )(panel)


def product_kernel(ids, panel, own, sib, keep, send):
    core = ids[2]
    upper = ids[3] == 0
    for k in range(8):
        total = None
        for source, blocks in ((core, own), (1 - core, sib)):
            left = []
            for p in range(2):
                part = panel[:, source, :, p, k].astype(F32)
                left.append(jnp.swapaxes(part, 0, 1).reshape(256, 128).astype(BF))
            re = blocks[0, k]
            im = blocks[1, k]
            form = (((0,), (0,)), ((), ()))
            one = lax.dot_general(
                left[0], jnp.concatenate([re, im], axis=1), form, preferred_element_type=F32
            )
            two = lax.dot_general(
                left[1], jnp.concatenate([-im, re], axis=1), form, preferred_element_type=F32
            )
            both = one + two
            total = both if total is None else total + both
        low = total[:64]
        high = total[64:]
        mine = jnp.where(upper, low, high)
        other = jnp.where(upper, high, low)
        for p in range(2):
            keep[p, k] = mine[:, 128 * p : 128 * p + 128]
            send[p, k] = other[:, 128 * p : 128 * p + 128]


def products(ids, panel, own, sib):
    half = jax.ShapeDtypeStruct((2, 8, 64, 128), F32)
    return pl.pallas_call(
        product_kernel,
        in_specs=[pl.BlockSpec(memory_space=pltpu.SMEM)] + whole(3),
        out_specs=whole(2),
        out_shape=[half, half],
        compiler_params=params(),
    )(ids, panel, own, sib)


def diag_kernel(keep, got, below, total, out):
    for k in range(8):
        sums = [keep[p, k] + got[p, k] for p in range(2)]
        for p in range(2):
            for z in range(4):
                total[z, p, k] = sums[p][16 * z : 16 * z + 16]
        left = []
        for value in sums:
            high = value.astype(BF)
            left.append(high)
            left.append((value - high.astype(F32)).astype(BF))
        left = jnp.concatenate(left, axis=1)
        panel = []
        for p in range(2):
            part = below[:, :, :, p, k].astype(F32)
            part = part.reshape(2, 2, 2, 2, 8, 256).transpose(3, 1, 2, 0, 4, 5)
            panel.append(part.reshape(128, 256).astype(BF))
        re, im = panel
        right_re = jnp.concatenate([re, re, -im, -im], axis=0)
        right_im = jnp.concatenate([im, im, re, re], axis=0)
        out[k] = jnp.dot(left, right_re, preferred_element_type=F32)
        out[8 + k] = jnp.dot(left, right_im, preferred_element_type=F32)


def diag_terms(keep, got, below):
    return pl.pallas_call(
        diag_kernel,
        in_specs=whole(3),
        out_specs=whole(2),
        out_shape=[
            jax.ShapeDtypeStruct((4, 2, 8, 16, 128), F32),
            jax.ShapeDtypeStruct((16, 64, 256), F32),
        ],
        compiler_params=params(),
    )(keep, got, below)


def spread(value, axes, size):
    copies = jnp.broadcast_to(value[None], (size,) + value.shape)
    return lax.all_to_all(copies, axes, 0, 0, tiled=True)


def shards(inverse_anc, lower_panel, diag_inverse, structure):
    my_row = lax.axis_index(ROW)
    my_col = lax.axis_index(COL)
    ids = jnp.stack([my_row, my_col, lax.axis_index("core"), lax.axis_index("zc")]).astype(jnp.int32)
    own = lower_panel.reshape(2, 8, 8, 256)

    lanes = split_lanes(own)
    lanes = lax.all_to_all(lanes.reshape(4, 2, 8, 8, 128), ("core", "zh"), 0, 0, tiled=True)
    lanes = lanes.reshape(2, 2, 2, 8, 8, 128)
    panel = spread(lanes, PLANE, 16)

    far = pick_far_half(inverse_anc, structure, ids)
    got = lax.ppermute(far, "h", [(0, 1), (1, 0)])
    mine = merge_halves(inverse_anc, got, structure, ids)
    sib = lax.ppermute(mine, "core", [(0, 1), (1, 0)])

    moves = []
    for q in range(16):
        for h in range(2):
            for m in range(16):
                moves.append((q * 32 + 16 * h + m, m * 32 + 2 * q + h))
    below = lax.ppermute(own, ROW + COL, moves)
    below = spread(below, "za", 2)
    below = spread(below, ("zb", "zc"), 4)
    below = spread(below.reshape(8, 2, 8, 8, 256), "core", 2)
    below = below.reshape(2, 4, 2, 2, 8, 8, 256)

    keep, send = products(ids, panel, mine, sib)
    summed = lax.ppermute(send, "zc", [(0, 1), (1, 0)])
    total, terms = diag_terms(keep, summed, below)

    terms = lax.all_to_all(terms, PLANE, 0, 0, tiled=True)
    part = jnp.sum(terms, axis=0).reshape(4, 1, 16, 256)
    part = jnp.broadcast_to(part, (4, 2, 16, 256)).reshape(8, 16, 256)
    part = lax.all_to_all(part, ("za", "zb", "zh"), 0, 0, tiled=True)
    place = lax.axis_index(PLANE)
    start = lax.dynamic_index_in_dim(diag_inverse.reshape(16, 16, 256), place, 0, keepdims=False)
    diag = spread(start + jnp.sum(part, axis=0), PLANE, 16)
    diag_block = diag.reshape(2, 8, 16, 256)

    rows = lax.all_to_all(total, ("za", "zb"), 0, 0, tiled=True)
    half = (-jnp.sum(rows, axis=0)).astype(BF)
    pair = spread(half, "h", 2)
    block = jnp.concatenate([pair[0], pair[1]], axis=-1)
    slots = lax.dynamic_index_in_dim(structure, my_col // 2, 1, keepdims=False)
    pieces = []
    for column in range(2):
        keep_it = (slots == 2 * my_col + column)[None, :, None, None]
        pieces.append(jnp.where(keep_it, block, jnp.zeros_like(block)))
    upper_inverse = jnp.concatenate(pieces, axis=3)
    return upper_inverse, diag_block


def solution(mesh):
    fine = Mesh(mesh.devices.reshape(2, 2, 2, 2, 2, 4, 2, 2), ROW + COL)
    placed = (
        P(None, ROW, COL),
        P(None, None, ROW, COL, None),
        P(None, None, ROW, None),
        P(),
    )
    return jax.shard_map(
        shards,
        mesh=fine,
        in_specs=placed,
        out_specs=(P(None, None, ROW, COL), P(None, None, ROW, None)),
        check_vma=False,
    )
```

```python
import jax
import jax.numpy as jnp
from jax import lax
from jax.experimental import pallas as pl
from jax.experimental.pallas import tpu as pltpu
from jax.sharding import Mesh, PartitionSpec as P

BF = jnp.bfloat16
F32 = jnp.float32
ROW = ("za", "zb", "zc", "core")
COL = ("zh", "y", "xa", "h")
PLANE = ("y", "xa", "h")
VMEM_LIMIT = 48 * 1024 * 1024


def params():
    return pltpu.CompilerParams(vmem_limit_bytes=VMEM_LIMIT)


def whole(count):
    return [pl.BlockSpec(memory_space=pltpu.VMEM)] * count


def block_row(k, st, ids):
    return st[k, ids[0]] - 4 * ids[0]


def block_col(k, st, ids):
    return lax.rem(st[k, ids[1] // 2], 2)


def present(k, st, ids):
    return st[k, ids[1] // 2] // 2 == ids[1]


def pick_kernel(st, ids, block, out):
    out[:, 0] = jnp.where(present(pl.program_id(0), st, ids), block[...], 0)


def pick_blocks(inverse_anc, structure, ids):
    def at(k, st, ids):
        return (0, block_row(k, st, ids), block_col(k, st, ids))

    return pl.pallas_call(
        pick_kernel,
        grid_spec=pltpu.PrefetchScalarGridSpec(
            num_scalar_prefetch=2,
            grid=(8,),
            in_specs=[pl.BlockSpec((2, 256, 256), at)],
            out_specs=pl.BlockSpec((2, 1, 256, 256), lambda k, st, ids: (0, k, 0, 0)),
        ),
        out_shape=jax.ShapeDtypeStruct((2, 8, 256, 256), BF),
        compiler_params=params(),
    )(structure, ids, inverse_anc)


def lanes_kernel(panel, out):
    x = panel[...].astype(F32).reshape(128, 256).astype(BF)
    src = lax.broadcasted_iota(jnp.int32, (256, 256), 0)
    dst = lax.broadcasted_iota(jnp.int32, (256, 256), 1)
    t = src % 16
    core = (src // 16) % 2
    zc = (src // 32) % 2
    zb = (src // 64) % 2
    za = src // 128
    place = core * 128 + zc * 64 + za * 32 + zb * 16 + t
    perm = jnp.where(place == dst, 1.0, 0.0).astype(BF)
    y = jnp.dot(x, perm, preferred_element_type=F32)
    for c in range(2):
        half = y[:, 128 * c : 128 * c + 128].reshape(2, 8, 8, 128).astype(BF)
        for z in range(16):
            out[c, z] = half


def split_lanes(panel):
    return pl.pallas_call(
        lanes_kernel,
        in_specs=whole(1),
        out_specs=whole(1)[0],
        out_shape=jax.ShapeDtypeStruct((2, 16, 2, 8, 8, 128), BF),
        compiler_params=params(),
    )(panel)


def product_kernel(ids, near, far, own, sib, out):
    core = ids[2]
    zh = ids[4]
    form = (((0,), (0,)), ((), ()))
    for k in range(8):
        total = None
        for source, blocks in ((core, own), (1 - core, sib)):
            left = []
            for p in range(2):
                parts = []
                for panel in (near, far):
                    parts.append(panel[source, :, p, k].astype(F32).reshape(128, 128))
                lower = jnp.where(zh == 0, parts[0], parts[1])
                upper = jnp.where(zh == 0, parts[1], parts[0])
                left.append(jnp.concatenate([lower, upper], axis=0).astype(BF))
            re = blocks[0, k]
            im = blocks[1, k]
            one = lax.dot_general(
                left[0], jnp.concatenate([re, im], axis=1), form, preferred_element_type=F32
            )
            two = lax.dot_general(
                left[1], jnp.concatenate([-im, re], axis=1), form, preferred_element_type=F32
            )
            both = one + two
            total = both if total is None else total + both
        for z in range(2):
            for h in range(2):
                for p in range(2):
                    at = 256 * p + 128 * h
                    out[2 * z + h, p, k] = total[64 * z : 64 * z + 64, at : at + 128]


def products(ids, near, far, own, sib):
    return pl.pallas_call(
        product_kernel,
        in_specs=[pl.BlockSpec(memory_space=pltpu.SMEM)] + whole(4),
        out_specs=whole(1)[0],
        out_shape=jax.ShapeDtypeStruct((4, 2, 8, 64, 128), F32),
        compiler_params=params(),
    )(ids, near, far, own, sib)


def diag_kernel(ids, parts, below, *outs):
    row = ids[0]
    zab = 2 * ids[6] + ids[5]
    out = outs[4]
    for k in range(8):
        sums = []
        for p in range(2):
            value = (parts[0, p, k] + parts[1, p, k]) + (parts[2, p, k] + parts[3, p, k])
            sums.append(value)
            quarters = [value[16 * i : 16 * i + 16] for i in range(4)]
            for i in range(4):
                rows = quarters[i]
                for mine in range(1, 4):
                    rows = jnp.where(zab == mine, quarters[i ^ mine], rows)
                outs[i][p, k] = rows
        left = []
        for value in sums:
            high = value.astype(BF)
            left.append(high)
            left.append((value - high.astype(F32)).astype(BF))
        left = jnp.concatenate(left, axis=1)
        panel = []
        for p in range(2):
            part = []
            for m in range(16):
                far = jnp.bitwise_xor(row, m)
                at = (far % 2) * 8 + (far // 2 % 2) * 4 + (far // 4 % 2) * 2 + far // 8
                part.append(below[at, p, k].astype(F32))
            panel.append(jnp.concatenate(part, axis=0).astype(BF))
        re, im = panel
        right_re = jnp.concatenate([re, re, -im, -im], axis=0)
        right_im = jnp.concatenate([im, im, re, re], axis=0)
        out[k] = jnp.dot(left, right_re, preferred_element_type=F32)
        out[8 + k] = jnp.dot(left, right_im, preferred_element_type=F32)


def diag_terms(ids, parts, below):
    quarter = jax.ShapeDtypeStruct((2, 8, 16, 128), F32)
    return pl.pallas_call(
        diag_kernel,
        in_specs=[pl.BlockSpec(memory_space=pltpu.SMEM)] + whole(2),
        out_specs=whole(5),
        out_shape=[quarter] * 4 + [jax.ShapeDtypeStruct((16, 64, 256), F32)],
        compiler_params=params(),
    )(ids, parts, below)


def spread(value, axes, size):
    copies = jnp.broadcast_to(value[None], (size,) + value.shape)
    return lax.all_to_all(copies, axes, 0, 0, tiled=True)


PAIR = [(0, 1), (1, 0)]


def doubled(value, axis):
    return jnp.concatenate([value, lax.ppermute(value, axis, PAIR)], axis=0)


def shards(inverse_anc, lower_panel, diag_inverse, structure):
    my_row = lax.axis_index(ROW)
    my_col = lax.axis_index(COL)
    ids = [my_row, my_col] + [lax.axis_index(axis) for axis in ("core", "zc", "zh", "zb", "za")]
    ids = jnp.stack(ids).astype(jnp.int32)
    own = lower_panel.reshape(2, 8, 8, 256)
    tie = lax.optimization_barrier

    moves = []
    for q in range(16):
        for h in range(2):
            for m in range(16):
                moves.append((q * 32 + 16 * h + m, m * 32 + 2 * q + h))
    below = lax.ppermute(own, ROW + COL, moves).reshape(1, 2, 8, 8, 256)

    group = ("core",) + PLANE
    other = lax.ppermute(own, "zh", PAIR)
    lanes = split_lanes(own)
    near = lax.all_to_all(lanes.reshape(32, 2, 8, 8, 128), group, 0, 0, tiled=True)

    other, near, below = tie((other, near, below))
    lanes = split_lanes(other)
    far = lax.all_to_all(lanes.reshape(32, 2, 8, 8, 128), group, 0, 0, tiled=True)

    mine = pick_blocks(inverse_anc, structure, ids)
    sib = lax.ppermute(mine, "core", PAIR)
    below = doubled(below, "za")
    below = doubled(below, "zb")
    far, below = tie((far, below))
    near = near.reshape(2, 16, 2, 8, 8, 128)
    far = far.reshape(2, 16, 2, 8, 8, 128)
    parts = products(ids, near, far, mine, sib)
    parts = lax.all_to_all(parts, ("zc", "h"), 0, 0, tiled=True)
    below = doubled(below, "zc")
    below = doubled(below, "core")
    rows, by_zb, by_za, by_both, terms = diag_terms(ids, parts, below)

    terms = lax.all_to_all(terms, PLANE, 0, 0, tiled=True)
    by_za = lax.ppermute(by_za, "za", PAIR)
    by_zb = lax.ppermute(by_zb, "zb", PAIR)
    by_both = lax.ppermute(by_both, ("za", "zb"), [(0, 3), (1, 2), (2, 1), (3, 0)])
    terms, by_za, by_zb, by_both = tie((terms, by_za, by_zb, by_both))
    half = (-((rows + by_za) + (by_zb + by_both))).astype(BF)
    part = jnp.sum(terms, axis=0).reshape(4, 1, 16, 256)
    part = jnp.broadcast_to(part, (4, 2, 16, 256)).reshape(8, 16, 256)
    part = lax.all_to_all(part, ("za", "zb", "zh"), 0, 0, tiled=True)
    place = lax.axis_index(PLANE)
    start = lax.dynamic_index_in_dim(diag_inverse.reshape(16, 16, 256), place, 0, keepdims=False)
    diag = spread(start + jnp.sum(part, axis=0), PLANE, 16)
    diag_block = diag.reshape(2, 8, 16, 256)

    partner = lax.ppermute(half, "h", PAIR)
    first = my_col % 2 == 0
    left = jnp.where(first, half, partner)
    right = jnp.where(first, partner, half)
    block = jnp.concatenate([left, right], axis=-1)
    slots = lax.dynamic_index_in_dim(structure, my_col // 2, 1, keepdims=False)
    pieces = []
    for column in range(2):
        keep_it = (slots == 2 * my_col + column)[None, :, None, None]
        pieces.append(jnp.where(keep_it, block, jnp.zeros_like(block)))
    upper_inverse = jnp.concatenate(pieces, axis=3)
    return upper_inverse, diag_block


def solution(mesh):
    fine = Mesh(mesh.devices.reshape(2, 2, 2, 2, 2, 4, 2, 2), ROW + COL)
    placed = (
        P(None, ROW, COL),
        P(None, None, ROW, COL, None),
        P(None, None, ROW, None),
        P(),
    )
    return jax.shard_map(
        shards,
        mesh=fine,
        in_specs=placed,
        out_specs=(P(None, None, ROW, COL), P(None, None, ROW, None)),
        check_vma=False,
    )
```

```python
import jax
import jax.numpy as jnp
from jax import lax
from jax.experimental import pallas as pl
from jax.experimental.pallas import tpu as pltpu
from jax.sharding import Mesh, PartitionSpec as P

BF = jnp.bfloat16
F32 = jnp.float32
F16 = jnp.float16
ROW = ("za", "zb", "zc", "core")
COL = ("zh", "y", "xa", "h")
PLANE = ("y", "xa", "h")
VMEM_LIMIT = 48 * 1024 * 1024


def params():
    return pltpu.CompilerParams(vmem_limit_bytes=VMEM_LIMIT)


def whole(count):
    return [pl.BlockSpec(memory_space=pltpu.VMEM)] * count


def block_row(k, st, ids):
    return st[k, ids[0]] - 4 * ids[0]


def block_col(k, st, ids):
    return lax.rem(st[k, ids[1] // 2], 2)


def present(k, st, ids):
    return st[k, ids[1] // 2] // 2 == ids[1]


def pick_kernel(st, ids, block, out):
    out[:, 0] = jnp.where(present(pl.program_id(0), st, ids), block[...], 0)


def pick_blocks(inverse_anc, structure, ids):
    def at(k, st, ids):
        return (0, block_row(k, st, ids), block_col(k, st, ids))

    return pl.pallas_call(
        pick_kernel,
        grid_spec=pltpu.PrefetchScalarGridSpec(
            num_scalar_prefetch=2,
            grid=(8,),
            in_specs=[pl.BlockSpec((2, 256, 256), at)],
            out_specs=pl.BlockSpec((2, 1, 256, 256), lambda k, st, ids: (0, k, 0, 0)),
        ),
        out_shape=jax.ShapeDtypeStruct((2, 8, 256, 256), BF),
        compiler_params=params(),
    )(structure, ids, inverse_anc)


def lanes_kernel(panel, out):
    x = panel[...].astype(F32).reshape(128, 256).astype(BF)
    src = lax.broadcasted_iota(jnp.int32, (256, 256), 0)
    dst = lax.broadcasted_iota(jnp.int32, (256, 256), 1)
    t = src % 16
    core = (src // 16) % 2
    zc = (src // 32) % 2
    zb = (src // 64) % 2
    za = src // 128
    place = core * 128 + zc * 64 + za * 32 + zb * 16 + t
    perm = jnp.where(place == dst, 1.0, 0.0).astype(BF)
    y = jnp.dot(x, perm, preferred_element_type=F32)
    for c in range(2):
        half = y[:, 128 * c : 128 * c + 128].reshape(2, 8, 8, 128).astype(BF)
        for z in range(16):
            out[c, z] = half


def split_lanes(panel):
    return pl.pallas_call(
        lanes_kernel,
        in_specs=whole(1),
        out_specs=whole(1)[0],
        out_shape=jax.ShapeDtypeStruct((2, 16, 2, 8, 8, 128), BF),
        compiler_params=params(),
    )(panel)


def product_kernel(ids, near, far, own, sib, out):
    core = ids[2]
    zh = ids[4]
    form = (((0,), (0,)), ((), ()))
    largest = jnp.zeros((8, 128), F32)
    for k in range(8):
        total = None
        for source, blocks in ((core, own), (1 - core, sib)):
            left = []
            for p in range(2):
                parts = []
                for panel in (near, far):
                    parts.append(panel[source, :, p, k].astype(F32).reshape(128, 128))
                lower = jnp.where(zh == 0, parts[0], parts[1])
                upper = jnp.where(zh == 0, parts[1], parts[0])
                left.append(jnp.concatenate([lower, upper], axis=0).astype(BF))
            re = blocks[0, k]
            im = blocks[1, k]
            one = lax.dot_general(
                left[0], jnp.concatenate([re, im], axis=1), form, preferred_element_type=F32
            )
            two = lax.dot_general(
                left[1], jnp.concatenate([-im, re], axis=1), form, preferred_element_type=F32
            )
            both = one + two
            total = both if total is None else total + both
        size = jnp.max(jnp.abs(total).reshape(16, 8, 512), axis=0)
        for lane in range(4):
            largest = jnp.maximum(largest, size[:, 128 * lane : 128 * lane + 128])
        for zc in range(2):
            for h in range(2):
                for zab in range(4):
                    for p in range(2):
                        row = 64 * zc + 16 * zab
                        lane = 256 * p + 128 * h
                        to = ((2 * zab + p) * 8 + k) * 16
                        out[2 * zc + h, to : to + 16] = total[row : row + 16, lane : lane + 128]
    largest = jnp.max(jnp.max(largest, axis=0, keepdims=True), axis=1, keepdims=True)
    power = jnp.clip(jnp.ceil(jnp.log2(largest)), -100.0, 100.0)
    scale = jnp.exp2(14.0 - power)
    for chunk in range(4):
        out[chunk, :1024] = out[chunk, :1024] * scale
        out[chunk, 1024:] = jnp.broadcast_to(power, (16, 128))


def products(ids, near, far, own, sib):
    return pl.pallas_call(
        product_kernel,
        in_specs=[pl.BlockSpec(memory_space=pltpu.SMEM)] + whole(4),
        out_specs=whole(1)[0],
        out_shape=jax.ShapeDtypeStruct((4, 1040, 128), F32),
        compiler_params=params(),
    )(ids, near, far, own, sib)


def diag_kernel(ids, summed, below, half, out):
    row = ids[0]
    for k in range(8):
        left = []
        for p in range(2):
            upper = (-summed[p, k]).astype(BF)
            half[p, k] = upper
            left.append(upper)
        left = jnp.concatenate(left, axis=1)
        panel = []
        for p in range(2):
            part = []
            for m in range(16):
                far = jnp.bitwise_xor(row, m)
                at = (far % 2) * 8 + (far // 2 % 2) * 4 + (far // 4 % 2) * 2 + far // 8
                part.append(below[at, p, k].astype(F32))
            panel.append(jnp.concatenate(part, axis=0).astype(BF))
        re, im = panel
        right_re = jnp.concatenate([re, -im], axis=0)
        right_im = jnp.concatenate([im, re], axis=0)
        out[k] = jnp.dot(left, right_re, preferred_element_type=F32)
        out[8 + k] = jnp.dot(left, right_im, preferred_element_type=F32)


def diag_terms(ids, summed, below):
    return pl.pallas_call(
        diag_kernel,
        in_specs=[pl.BlockSpec(memory_space=pltpu.SMEM)] + whole(2),
        out_specs=whole(2),
        out_shape=[
            jax.ShapeDtypeStruct((2, 8, 16, 128), BF),
            jax.ShapeDtypeStruct((16, 16, 256), F32),
        ],
        compiler_params=params(),
    )(ids, summed, below)


PAIR = [(0, 1), (1, 0)]


def doubled(value, axis):
    return jnp.concatenate([value, lax.ppermute(value, axis, PAIR)], axis=0)


def shards(inverse_anc, lower_panel, diag_inverse, structure):
    my_row = lax.axis_index(ROW)
    my_col = lax.axis_index(COL)
    ids = [my_row, my_col] + [lax.axis_index(axis) for axis in ("core", "zc", "zh", "zb", "za")]
    ids = jnp.stack(ids).astype(jnp.int32)
    own = lower_panel.reshape(2, 8, 8, 256)
    tie = lax.optimization_barrier

    moves = []
    for q in range(16):
        for h in range(2):
            for m in range(16):
                moves.append((q * 32 + 16 * h + m, m * 32 + 2 * q + h))

    group = ("core",) + PLANE
    other = lax.ppermute(own, "zh", PAIR)
    lanes = split_lanes(own)
    near = lax.all_to_all(lanes.reshape(32, 2, 8, 8, 128), group, 0, 0, tiled=True)

    mine = pick_blocks(inverse_anc, structure, ids)
    sib = lax.ppermute(mine, "core", PAIR)
    other, near, mine = tie((other, near, mine))
    lanes = split_lanes(other)
    far = lax.all_to_all(lanes.reshape(32, 2, 8, 8, 128), group, 0, 0, tiled=True)
    own = tie((own, lanes))[0]
    below = lax.ppermute(own, ROW + COL, moves).reshape(1, 2, 8, 8, 256)
    below = doubled(below, "za")
    far, below = tie((far, below))

    near = near.reshape(2, 16, 2, 8, 8, 128)
    far = far.reshape(2, 16, 2, 8, 8, 128)
    parts = products(ids, near, far, mine, sib)
    below, parts = tie((below, parts))
    below = doubled(below, "zb")
    got = lax.all_to_all(parts.astype(F16), ("zc", "h"), 0, 0, tiled=True).astype(F32)
    power = got[:, 1024:1025]
    most = jnp.max(power, axis=0, keepdims=True) + 2.0
    parts = jnp.sum(got[:, :1024] * jnp.exp2(power - most), axis=0).reshape(4, 256, 128)
    parts = jnp.concatenate([parts, jnp.broadcast_to(most, (4, 16, 128))], axis=1)

    below, parts = tie((below, parts))
    below = doubled(below, "zc")
    below = doubled(below, "core")
    got = lax.all_to_all(parts.astype(F16), ("za", "zb"), 0, 0, tiled=True).astype(F32)
    summed = jnp.sum(got[:, :256] * jnp.exp2(got[:, 256:257] - 14.0), axis=0)
    half, terms = diag_terms(ids, summed.reshape(2, 8, 16, 128), below)

    terms = lax.all_to_all(terms, PLANE, 0, 0, tiled=True)
    partner = lax.ppermute(half, "h", PAIR)
    terms, partner = tie((terms, partner))
    part = jnp.sum(terms, axis=0)
    part = part + lax.ppermute(part, "zh", PAIR)
    place = lax.axis_index(PLANE)
    start = lax.dynamic_index_in_dim(diag_inverse.reshape(16, 16, 256), place, 0, keepdims=False)
    diag = jnp.broadcast_to((start - part)[None], (16, 16, 256))
    diag = lax.all_to_all(diag, PLANE, 0, 0, tiled=True)
    diag_block = diag.reshape(2, 8, 16, 256)

    first = my_col % 2 == 0
    left = jnp.where(first, half, partner)
    right = jnp.where(first, partner, half)
    block = jnp.concatenate([left, right], axis=-1)
    slots = lax.dynamic_index_in_dim(structure, my_col // 2, 1, keepdims=False)
    pieces = []
    for column in range(2):
        keep_it = (slots == 2 * my_col + column)[None, :, None, None]
        pieces.append(jnp.where(keep_it, block, jnp.zeros_like(block)))
    upper_inverse = jnp.concatenate(pieces, axis=3)
    return upper_inverse, diag_block


def solution(mesh):
    fine = Mesh(mesh.devices.reshape(2, 2, 2, 2, 2, 4, 2, 2), ROW + COL)
    placed = (
        P(None, ROW, COL),
        P(None, None, ROW, COL, None),
        P(None, None, ROW, None),
        P(),
    )
    return jax.shard_map(
        shards,
        mesh=fine,
        in_specs=placed,
        out_specs=(P(None, None, ROW, COL), P(None, None, ROW, None)),
        check_vma=False,
    )
```

```python
import jax
import jax.numpy as jnp
from jax import lax
from jax.experimental import pallas as pl
from jax.experimental.pallas import tpu as pltpu
from jax.sharding import Mesh, PartitionSpec as P

BF = jnp.bfloat16
F32 = jnp.float32
F16 = jnp.float16
ROW = ("za", "zb", "zc", "core")
COL = ("zh", "y", "xa", "h")
PLANE = ("y", "xa", "h")
VMEM_LIMIT = 48 * 1024 * 1024


def params():
    return pltpu.CompilerParams(vmem_limit_bytes=VMEM_LIMIT)


def whole(count):
    return [pl.BlockSpec(memory_space=pltpu.VMEM)] * count


def block_row(k, st, ids):
    return st[k, ids[0]] - 4 * ids[0]


def block_col(k, st, ids):
    return lax.rem(st[k, ids[1] // 2], 2)


def present(k, st, ids):
    return st[k, ids[1] // 2] // 2 == ids[1]


def pick_kernel(st, ids, blocks, out, sem):
    copies = []
    for k in range(8):
        rows = pl.ds(pl.multiple_of(256 * block_row(k, st, ids), 256), 256)
        lanes = pl.ds(pl.multiple_of(256 * block_col(k, st, ids), 256), 256)
        copies.append(pltpu.make_async_copy(blocks.at[:, rows, lanes], out.at[:, k], sem.at[k]))
        copies[-1].start()
    for copy in copies:
        copy.wait()


def pick_blocks(inverse_anc, structure, ids):
    return pl.pallas_call(
        pick_kernel,
        in_specs=[pl.BlockSpec(memory_space=pltpu.SMEM)] * 2 + [pl.BlockSpec(memory_space=pl.ANY)],
        out_specs=pl.BlockSpec(memory_space=pl.ANY),
        out_shape=jax.ShapeDtypeStruct((2, 8, 256, 256), BF),
        scratch_shapes=[pltpu.SemaphoreType.DMA((8,))],
        compiler_params=params(),
    )(structure, ids, inverse_anc)


def lanes_kernel(panel, out):
    x = panel[...].astype(F32).reshape(128, 256).astype(BF)
    src = lax.broadcasted_iota(jnp.int32, (256, 256), 0)
    dst = lax.broadcasted_iota(jnp.int32, (256, 256), 1)
    t = src % 16
    core = (src // 16) % 2
    zc = (src // 32) % 2
    zb = (src // 64) % 2
    za = src // 128
    place = core * 128 + zc * 64 + za * 32 + zb * 16 + t
    perm = jnp.where(place == dst, 1.0, 0.0).astype(BF)
    y = jnp.dot(x, perm, preferred_element_type=F32)
    for c in range(2):
        half = y[:, 128 * c : 128 * c + 128].reshape(2, 8, 8, 128).astype(BF)
        for z in range(16):
            out[c, z] = half


def split_lanes(panel):
    return pl.pallas_call(
        lanes_kernel,
        in_specs=whole(1),
        out_specs=whole(1)[0],
        out_shape=jax.ShapeDtypeStruct((2, 16, 2, 8, 8, 128), BF),
        compiler_params=params(),
    )(panel)


def product_kernel(st, ids, near, far, own, sib, out):
    core = ids[2]
    zh = ids[4]
    form = (((0,), (0,)), ((), ()))
    largest = jnp.zeros((8, 128), F32)
    for k in range(8):
        total = None
        for source, blocks in ((core, own), (1 - core, sib)):
            left = []
            for p in range(2):
                parts = []
                for panel in (near, far):
                    parts.append(panel[source, :, p, k].astype(F32).reshape(128, 128))
                lower = jnp.where(zh == 0, parts[0], parts[1])
                upper = jnp.where(zh == 0, parts[1], parts[0])
                left.append(jnp.concatenate([lower, upper], axis=0).astype(BF))
            re = blocks[0, k]
            im = blocks[1, k]
            one = lax.dot_general(
                left[0], jnp.concatenate([re, im], axis=1), form, preferred_element_type=F32
            )
            two = lax.dot_general(
                left[1], jnp.concatenate([-im, re], axis=1), form, preferred_element_type=F32
            )
            both = one + two
            total = both if total is None else total + both
        total = jnp.where(present(k, st, ids), total, 0.0)
        size = jnp.max(jnp.abs(total).reshape(16, 8, 512), axis=0)
        for lane in range(4):
            largest = jnp.maximum(largest, size[:, 128 * lane : 128 * lane + 128])
        for zc in range(2):
            for h in range(2):
                for zab in range(4):
                    for p in range(2):
                        row = 64 * zc + 16 * zab
                        lane = 256 * p + 128 * h
                        to = ((2 * zab + p) * 8 + k) * 16
                        out[2 * zc + h, to : to + 16] = total[row : row + 16, lane : lane + 128]
    largest = jnp.max(jnp.max(largest, axis=0, keepdims=True), axis=1, keepdims=True)
    power = jnp.clip(jnp.ceil(jnp.log2(largest)), -100.0, 100.0)
    scale = jnp.exp2(14.0 - power)
    for chunk in range(4):
        out[chunk, :1024] = out[chunk, :1024] * scale
        out[chunk, 1024:] = jnp.broadcast_to(power, (16, 128))


def products(structure, ids, near, far, own, sib):
    return pl.pallas_call(
        product_kernel,
        in_specs=[pl.BlockSpec(memory_space=pltpu.SMEM)] * 2 + whole(4),
        out_specs=whole(1)[0],
        out_shape=jax.ShapeDtypeStruct((4, 1040, 128), F32),
        compiler_params=params(),
    )(structure, ids, near, far, own, sib)


def diag_kernel(ids, summed, below, half, out):
    row = ids[0]
    for k in range(8):
        left = []
        for p in range(2):
            upper = (-summed[p, k]).astype(BF)
            half[p, k] = upper
            left.append(upper)
        left = jnp.concatenate(left, axis=1)
        panel = []
        for p in range(2):
            part = []
            for m in range(16):
                far = jnp.bitwise_xor(row, m)
                at = (far % 2) * 8 + (far // 2 % 2) * 4 + (far // 4 % 2) * 2 + far // 8
                part.append(below[at, p, k].astype(F32))
            panel.append(jnp.concatenate(part, axis=0).astype(BF))
        re, im = panel
        right_re = jnp.concatenate([re, -im], axis=0)
        right_im = jnp.concatenate([im, re], axis=0)
        out[k] = jnp.dot(left, right_re, preferred_element_type=F32)
        out[8 + k] = jnp.dot(left, right_im, preferred_element_type=F32)


def diag_terms(ids, summed, below):
    return pl.pallas_call(
        diag_kernel,
        in_specs=[pl.BlockSpec(memory_space=pltpu.SMEM)] + whole(2),
        out_specs=whole(2),
        out_shape=[
            jax.ShapeDtypeStruct((2, 8, 16, 128), BF),
            jax.ShapeDtypeStruct((16, 16, 256), F32),
        ],
        compiler_params=params(),
    )(ids, summed, below)


PAIR = [(0, 1), (1, 0)]


def doubled(value, axis):
    return jnp.concatenate([value, lax.ppermute(value, axis, PAIR)], axis=0)


def shards(inverse_anc, lower_panel, diag_inverse, structure):
    my_row = lax.axis_index(ROW)
    my_col = lax.axis_index(COL)
    ids = [my_row, my_col] + [lax.axis_index(axis) for axis in ("core", "zc", "zh", "zb", "za")]
    ids = jnp.stack(ids).astype(jnp.int32)
    own = lower_panel.reshape(2, 8, 8, 256)
    tie = lax.optimization_barrier

    group = ("core",) + PLANE
    other = lax.ppermute(own, "zh", PAIR)
    lanes = split_lanes(own)
    near = lax.all_to_all(lanes.reshape(32, 2, 8, 8, 128), group, 0, 0, tiled=True)

    mine = pick_blocks(inverse_anc, structure, ids)
    sib = lax.ppermute(mine, "core", PAIR)
    other, near, mine = tie((other, near, mine))
    lanes = split_lanes(other)
    far = lax.all_to_all(lanes.reshape(32, 2, 8, 8, 128), group, 0, 0, tiled=True)

    own = tie((own, lanes))[0]
    below = []
    for flip in (0, 8):
        moves = []
        for q in range(16):
            for h in range(2):
                for m in range(16):
                    moves.append((q * 32 + 16 * h + m, (m ^ flip) * 32 + 2 * q + h))
        below.append(lax.ppermute(own, ROW + COL, moves))
    below = jnp.stack(below)
    far, below = tie((far, below))

    near = near.reshape(2, 16, 2, 8, 8, 128)
    far = far.reshape(2, 16, 2, 8, 8, 128)
    parts = products(structure, ids, near, far, mine, sib)
    below, parts = tie((below, parts))
    below = doubled(below, "zb")
    got = lax.all_to_all(parts.astype(F16), ("zc", "h"), 0, 0, tiled=True).astype(F32)
    power = got[:, 1024:1025]
    most = jnp.max(power, axis=0, keepdims=True) + 2.0
    parts = jnp.sum(got[:, :1024] * jnp.exp2(power - most), axis=0).reshape(4, 256, 128)
    parts = jnp.concatenate([parts, jnp.broadcast_to(most, (4, 16, 128))], axis=1).astype(F16)

    below, parts = tie((below, parts))
    below = doubled(below, "zc")
    below = doubled(below, "core")
    got = lax.all_to_all(parts, ("za", "zb"), 0, 0, tiled=True).astype(F32)
    summed = jnp.sum(got[:, :256] * jnp.exp2(got[:, 256:257] - 14.0), axis=0)
    half, terms = diag_terms(ids, summed.reshape(2, 8, 16, 128), below)

    terms = lax.all_to_all(terms, PLANE, 0, 0, tiled=True)
    partner = lax.ppermute(half, "h", PAIR)
    part = jnp.sum(terms, axis=0)
    part = part + lax.ppermute(part, "zh", PAIR)
    part, partner = tie((part, partner))
    place = lax.axis_index(PLANE)
    start = lax.dynamic_index_in_dim(diag_inverse.reshape(16, 16, 256), place, 0, keepdims=False)
    diag = jnp.broadcast_to((start - part)[None], (16, 16, 256))
    diag = lax.all_to_all(diag, PLANE, 0, 0, tiled=True)
    diag_block = diag.reshape(2, 8, 16, 256)

    first = my_col % 2 == 0
    left = jnp.where(first, half, partner)
    right = jnp.where(first, partner, half)
    block = jnp.concatenate([left, right], axis=-1)
    slots = lax.dynamic_index_in_dim(structure, my_col // 2, 1, keepdims=False)
    pieces = []
    for column in range(2):
        keep_it = (slots == 2 * my_col + column)[None, :, None, None]
        pieces.append(jnp.where(keep_it, block, jnp.zeros_like(block)))
    upper_inverse = jnp.concatenate(pieces, axis=3)
    return upper_inverse, diag_block


def solution(mesh):
    fine = Mesh(mesh.devices.reshape(2, 2, 2, 2, 2, 4, 2, 2), ROW + COL)
    placed = (
        P(None, ROW, COL),
        P(None, None, ROW, COL, None),
        P(None, None, ROW, None),
        P(),
    )
    return jax.shard_map(
        shards,
        mesh=fine,
        in_specs=placed,
        out_specs=(P(None, None, ROW, COL), P(None, None, ROW, None)),
        check_vma=False,
    )
```

```python
import jax
import jax.numpy as jnp
from jax import lax
from jax.experimental import pallas as pl
from jax.experimental.pallas import tpu as pltpu
from jax.sharding import Mesh, PartitionSpec as P

BF = jnp.bfloat16
F32 = jnp.float32
F16 = jnp.float16
ROW = ("za", "zb", "zc", "core")
COL = ("zh", "y", "xa", "h")
PLANE = ("y", "xa", "h")
VMEM_LIMIT = 48 * 1024 * 1024


def params():
    return pltpu.CompilerParams(vmem_limit_bytes=VMEM_LIMIT)


def whole(count):
    return [pl.BlockSpec(memory_space=pltpu.VMEM)] * count


def present(k, st, ids):
    return st[k, ids[1] // 2] // 2 == ids[1]


def block_at(k, row, st, ids):
    down = 256 * (st[k, row] - 4 * row)
    right = 256 * lax.rem(st[k, ids[1] // 2], 2)
    return down, right


def lanes_kernel(panel, out):
    x = panel[...].astype(F32).reshape(128, 256).astype(BF)
    src = lax.broadcasted_iota(jnp.int32, (256, 256), 0)
    dst = lax.broadcasted_iota(jnp.int32, (256, 256), 1)
    t = src % 16
    core = (src // 16) % 2
    zc = (src // 32) % 2
    zb = (src // 64) % 2
    za = src // 128
    place = core * 128 + zc * 64 + za * 32 + zb * 16 + t
    perm = jnp.where(place == dst, 1.0, 0.0).astype(BF)
    y = jnp.dot(x, perm, preferred_element_type=F32)
    for c in range(2):
        half = y[:, 128 * c : 128 * c + 128].reshape(2, 8, 8, 128).astype(BF)
        for z in range(16):
            out[c, z] = half


def split_lanes(panel):
    return pl.pallas_call(
        lanes_kernel,
        in_specs=whole(1),
        out_specs=whole(1)[0],
        out_shape=jax.ShapeDtypeStruct((2, 16, 2, 8, 8, 128), BF),
        compiler_params=params(),
    )(panel)


def product_kernel(st, ids, near, far, own, sib, out):
    core = ids[2]
    zh = ids[4]
    form = (((0,), (0,)), ((), ()))
    largest = jnp.zeros((8, 128), F32)
    for k in range(8):
        total = None
        for source, blocks in ((core, own), (1 - core, sib)):
            down, right = block_at(k, ids[0] - core + source, st, ids)
            left = []
            right_re, right_im = [], []
            for panel, half in ((near, zh), (far, 1 - zh)):
                rows = pl.ds(pl.multiple_of(down + 128 * half, 128), 128)
                lanes = pl.ds(pl.multiple_of(right, 256), 256)
                right_re.append(blocks[0, rows, lanes])
                right_im.append(blocks[1, rows, lanes])
            for p in range(2):
                parts = [panel[source, :, p, k].reshape(128, 128) for panel in (near, far)]
                left.append(jnp.concatenate(parts, axis=0))
            re = jnp.concatenate(right_re, axis=0)
            im = jnp.concatenate(right_im, axis=0)
            one = lax.dot_general(
                left[0], jnp.concatenate([re, im], axis=1), form, preferred_element_type=F32
            )
            two = lax.dot_general(
                left[1], jnp.concatenate([-im, re], axis=1), form, preferred_element_type=F32
            )
            both = one + two
            total = both if total is None else total + both
        total = jnp.where(present(k, st, ids), total, 0.0)
        size = jnp.max(jnp.abs(total).reshape(16, 8, 512), axis=0)
        for lane in range(4):
            largest = jnp.maximum(largest, size[:, 128 * lane : 128 * lane + 128])
        for zc in range(2):
            for h in range(2):
                for zab in range(4):
                    for p in range(2):
                        row = 64 * zc + 16 * zab
                        lane = 256 * p + 128 * h
                        to = ((2 * zab + p) * 8 + k) * 16
                        out[2 * zc + h, to : to + 16] = total[row : row + 16, lane : lane + 128]
    largest = jnp.max(jnp.max(largest, axis=0, keepdims=True), axis=1, keepdims=True)
    power = jnp.clip(jnp.ceil(jnp.log2(largest)), -100.0, 100.0)
    scale = jnp.exp2(14.0 - power)
    for chunk in range(4):
        out[chunk, :1024] = out[chunk, :1024] * scale
        out[chunk, 1024:] = jnp.broadcast_to(power, (16, 128))


def products(structure, ids, near, far, own, sib):
    return pl.pallas_call(
        product_kernel,
        in_specs=[pl.BlockSpec(memory_space=pltpu.SMEM)] * 2 + whole(4),
        out_specs=whole(1)[0],
        out_shape=jax.ShapeDtypeStruct((4, 1040, 128), F32),
        compiler_params=params(),
    )(structure, ids, near, far, own, sib)


def diag_kernel(ids, summed, below, half, out):
    row = ids[0]
    for k in range(8):
        left = []
        for p in range(2):
            upper = (-summed[p, k]).astype(BF)
            half[p, k] = upper
            left.append(upper)
        left = jnp.concatenate(left, axis=1)
        panel = []
        for p in range(2):
            part = []
            for m in range(16):
                far = jnp.bitwise_xor(row, m)
                at = (far % 2) * 8 + (far // 2 % 2) * 4 + (far // 4 % 2) * 2 + far // 8
                part.append(below[at, p, k].astype(F32))
            panel.append(jnp.concatenate(part, axis=0).astype(BF))
        re, im = panel
        right_re = jnp.concatenate([re, -im], axis=0)
        right_im = jnp.concatenate([im, re], axis=0)
        out[k] = jnp.dot(left, right_re, preferred_element_type=F32)
        out[8 + k] = jnp.dot(left, right_im, preferred_element_type=F32)


def diag_terms(ids, summed, below):
    return pl.pallas_call(
        diag_kernel,
        in_specs=[pl.BlockSpec(memory_space=pltpu.SMEM)] + whole(2),
        out_specs=whole(2),
        out_shape=[
            jax.ShapeDtypeStruct((2, 8, 16, 128), BF),
            jax.ShapeDtypeStruct((16, 16, 256), F32),
        ],
        compiler_params=params(),
    )(ids, summed, below)


def copies_kernel(start, part, other, out):
    value = start[...] - (part[...] + other[...])
    for chip in range(16):
        out[chip] = value


def diag_copies(start, part, other):
    return pl.pallas_call(
        copies_kernel,
        in_specs=whole(3),
        out_specs=whole(1)[0],
        out_shape=jax.ShapeDtypeStruct((16, 16, 256), F32),
        compiler_params=params(),
    )(start, part, other)


PAIR = [(0, 1), (1, 0)]


def doubled(value, axis):
    return jnp.concatenate([value, lax.ppermute(value, axis, PAIR)], axis=0)


def shards(inverse_anc, lower_panel, diag_inverse, structure):
    my_row = lax.axis_index(ROW)
    my_col = lax.axis_index(COL)
    ids = [my_row, my_col] + [lax.axis_index(axis) for axis in ("core", "zc", "zh", "zb", "za")]
    ids = jnp.stack(ids).astype(jnp.int32)
    own = lower_panel.reshape(2, 8, 8, 256)
    sib = lax.ppermute(inverse_anc, "core", PAIR)
    tie = lax.optimization_barrier

    group = ("core",) + PLANE
    other = lax.ppermute(own, "zh", PAIR)
    lanes = split_lanes(own)
    near = lax.all_to_all(lanes.reshape(32, 2, 8, 8, 128), group, 0, 0, tiled=True)

    other, near = tie((other, near))
    lanes = split_lanes(other)
    far = lax.all_to_all(lanes.reshape(32, 2, 8, 8, 128), group, 0, 0, tiled=True)

    own = tie((own, lanes))[0]
    below = []
    for flip in (0, 8):
        moves = []
        for q in range(16):
            for h in range(2):
                for m in range(16):
                    moves.append((q * 32 + 16 * h + m, (m ^ flip) * 32 + 2 * q + h))
        below.append(lax.ppermute(own, ROW + COL, moves))
    below = jnp.stack(below)
    far, below = tie((far, below))

    near = near.reshape(2, 16, 2, 8, 8, 128)
    far = far.reshape(2, 16, 2, 8, 8, 128)
    parts = products(structure, ids, near, far, inverse_anc, sib)
    below, parts = tie((below, parts))
    below = doubled(below, "zb")
    got = lax.all_to_all(parts.astype(F16), ("zc", "h"), 0, 0, tiled=True).astype(F32)
    power = got[:, 1024:1025]
    most = jnp.max(power, axis=0, keepdims=True) + 2.0
    parts = jnp.sum(got[:, :1024] * jnp.exp2(power - most), axis=0).reshape(4, 256, 128)
    parts = jnp.concatenate([parts, jnp.broadcast_to(most, (4, 16, 128))], axis=1).astype(F16)

    below, parts = tie((below, parts))
    below = doubled(below, "zc")
    below = doubled(below, "core")
    got = lax.all_to_all(parts, ("za", "zb"), 0, 0, tiled=True).astype(F32)
    summed = jnp.sum(got[:, :256] * jnp.exp2(got[:, 256:257] - 14.0), axis=0)
    half, terms = diag_terms(ids, summed.reshape(2, 8, 16, 128), below)

    terms = lax.all_to_all(terms, PLANE, 0, 0, tiled=True)
    partner = lax.ppermute(half, "h", PAIR)
    part = jnp.sum(terms, axis=0)
    other, partner = tie((lax.ppermute(part, "zh", PAIR), partner))
    place = lax.axis_index(PLANE)
    start = lax.dynamic_index_in_dim(diag_inverse.reshape(16, 16, 256), place, 0, keepdims=False)
    diag = diag_copies(start, part, other)
    diag = lax.all_to_all(diag, PLANE, 0, 0, tiled=True)
    diag_block = diag.reshape(2, 8, 16, 256)

    first = my_col % 2 == 0
    left = jnp.where(first, half, partner)
    right = jnp.where(first, partner, half)
    block = jnp.concatenate([left, right], axis=-1)
    slots = lax.dynamic_index_in_dim(structure, my_col // 2, 1, keepdims=False)
    pieces = []
    for column in range(2):
        keep_it = (slots == 2 * my_col + column)[None, :, None, None]
        pieces.append(jnp.where(keep_it, block, jnp.zeros_like(block)))
    upper_inverse = jnp.concatenate(pieces, axis=3)
    return upper_inverse, diag_block


def solution(mesh):
    fine = Mesh(mesh.devices.reshape(2, 2, 2, 2, 2, 4, 2, 2), ROW + COL)
    placed = (
        P(None, ROW, COL),
        P(None, None, ROW, COL, None),
        P(None, None, ROW, None),
        P(),
    )
    return jax.shard_map(
        shards,
        mesh=fine,
        in_specs=placed,
        out_specs=(P(None, None, ROW, COL), P(None, None, ROW, None)),
        check_vma=False,
    )
```

```python
import jax
import jax.numpy as jnp
from jax import lax
from jax.experimental import pallas as pl
from jax.experimental.pallas import tpu as pltpu
from jax.sharding import Mesh, PartitionSpec as P

BF = jnp.bfloat16
F32 = jnp.float32
F16 = jnp.float16
ROW = ("za", "zb", "zc", "core")
COL = ("zh", "y", "xa", "h")
PLANE = ("y", "xa", "h")
VMEM_LIMIT = 48 * 1024 * 1024


def params():
    return pltpu.CompilerParams(vmem_limit_bytes=VMEM_LIMIT)


def whole(count):
    return [pl.BlockSpec(memory_space=pltpu.VMEM)] * count


def present(k, st, ids):
    return st[k, ids[1] // 2] // 2 == ids[1]


def block_at(k, row, st, ids):
    down = 256 * (st[k, row] - 4 * row)
    right = 256 * lax.rem(st[k, ids[1] // 2], 2)
    return down, right


def lanes_kernel(panel, out):
    x = panel[...].astype(F32).reshape(128, 256).astype(BF)
    src = lax.broadcasted_iota(jnp.int32, (256, 256), 0)
    dst = lax.broadcasted_iota(jnp.int32, (256, 256), 1)
    t = src % 16
    core = (src // 16) % 2
    zc = (src // 32) % 2
    zb = (src // 64) % 2
    za = src // 128
    place = core * 128 + zc * 64 + za * 32 + zb * 16 + t
    perm = jnp.where(place == dst, 1.0, 0.0).astype(BF)
    y = jnp.dot(x, perm, preferred_element_type=F32)
    for c in range(2):
        half = y[:, 128 * c : 128 * c + 128].reshape(2, 8, 8, 128).astype(BF)
        for z in range(16):
            out[c, z] = half


def split_lanes(panel):
    return pl.pallas_call(
        lanes_kernel,
        in_specs=whole(1),
        out_specs=whole(1)[0],
        out_shape=jax.ShapeDtypeStruct((2, 16, 2, 8, 8, 128), BF),
        compiler_params=params(),
    )(panel)


def product_kernel(st, ids, near, far, own, sib, out):
    core = ids[2]
    zh = ids[4]
    form = (((0,), (0,)), ((), ()))
    largest = jnp.zeros((8, 128), F32)
    for k in range(8):
        total = None
        for source, blocks in ((core, own), (1 - core, sib)):
            down, right = block_at(k, ids[0] - core + source, st, ids)
            left = []
            right_re, right_im = [], []
            for panel, half in ((near, zh), (far, 1 - zh)):
                rows = pl.ds(pl.multiple_of(down + 128 * half, 128), 128)
                lanes = pl.ds(pl.multiple_of(right, 256), 256)
                right_re.append(blocks[0, rows, lanes])
                right_im.append(blocks[1, rows, lanes])
            for p in range(2):
                parts = [panel[source, :, p, k].reshape(128, 128) for panel in (near, far)]
                left.append(jnp.concatenate(parts, axis=0))
            re = jnp.concatenate(right_re, axis=0)
            im = jnp.concatenate(right_im, axis=0)
            one = lax.dot_general(
                left[0], jnp.concatenate([re, im], axis=1), form, preferred_element_type=F32
            )
            two = lax.dot_general(
                left[1], jnp.concatenate([-im, re], axis=1), form, preferred_element_type=F32
            )
            both = one + two
            total = both if total is None else total + both
        total = jnp.where(present(k, st, ids), total, 0.0)
        size = jnp.max(jnp.abs(total).reshape(16, 8, 512), axis=0)
        for lane in range(4):
            largest = jnp.maximum(largest, size[:, 128 * lane : 128 * lane + 128])
        for zc in range(2):
            for h in range(2):
                for zab in range(4):
                    for p in range(2):
                        row = 64 * zc + 16 * zab
                        lane = 256 * p + 128 * h
                        to = ((2 * zab + p) * 8 + k) * 16
                        out[2 * zc + h, to : to + 16] = total[row : row + 16, lane : lane + 128]
    largest = jnp.max(jnp.max(largest, axis=0, keepdims=True), axis=1, keepdims=True)
    power = jnp.clip(jnp.ceil(jnp.log2(largest)), -100.0, 100.0)
    scale = jnp.exp2(14.0 - power)
    for chunk in range(4):
        out[chunk, :1024] = out[chunk, :1024] * scale
        out[chunk, 1024:] = jnp.broadcast_to(power, (16, 128))


def products(structure, ids, near, far, own, sib):
    return pl.pallas_call(
        product_kernel,
        in_specs=[pl.BlockSpec(memory_space=pltpu.SMEM)] * 2 + whole(4),
        out_specs=whole(1)[0],
        out_shape=jax.ShapeDtypeStruct((4, 1040, 128), F32),
        compiler_params=params(),
    )(structure, ids, near, far, own, sib)


def diag_kernel(ids, summed, below, half, out):
    row = ids[0]
    for k in range(8):
        left = []
        for p in range(2):
            upper = (-summed[p, k]).astype(BF)
            half[p, k] = upper
            left.append(upper)
        left = jnp.concatenate(left, axis=1)
        panel = []
        for p in range(2):
            part = []
            for m in range(16):
                far = jnp.bitwise_xor(row, m)
                at = (far % 2) * 8 + (far // 2 % 2) * 4 + (far // 4 % 2) * 2 + far // 8
                part.append(below[at, p, k].astype(F32))
            panel.append(jnp.concatenate(part, axis=0).astype(BF))
        re, im = panel
        right_re = jnp.concatenate([re, -im], axis=0)
        right_im = jnp.concatenate([im, re], axis=0)
        out[k] = jnp.dot(left, right_re, preferred_element_type=F32)
        out[8 + k] = jnp.dot(left, right_im, preferred_element_type=F32)


def diag_terms(ids, summed, below):
    return pl.pallas_call(
        diag_kernel,
        in_specs=[pl.BlockSpec(memory_space=pltpu.SMEM)] + whole(2),
        out_specs=whole(2),
        out_shape=[
            jax.ShapeDtypeStruct((2, 8, 16, 128), BF),
            jax.ShapeDtypeStruct((16, 16, 256), F32),
        ],
        compiler_params=params(),
    )(ids, summed, below)


def copies_kernel(start, part, other, out):
    value = start[...] - (part[...] + other[...])
    for chip in range(16):
        out[chip] = value


def diag_copies(start, part, other):
    return pl.pallas_call(
        copies_kernel,
        in_specs=whole(3),
        out_specs=whole(1)[0],
        out_shape=jax.ShapeDtypeStruct((16, 16, 256), F32),
        compiler_params=params(),
    )(start, part, other)


PAIR = [(0, 1), (1, 0)]


def doubled(value, axis):
    return jnp.concatenate([value, lax.ppermute(value, axis, PAIR)], axis=0)


def shards(inverse_anc, lower_panel, diag_inverse, structure):
    my_row = lax.axis_index(ROW)
    my_col = lax.axis_index(COL)
    ids = [my_row, my_col] + [lax.axis_index(axis) for axis in ("core", "zc", "zh", "zb", "za")]
    ids = jnp.stack(ids).astype(jnp.int32)
    own = lower_panel.reshape(2, 8, 8, 256)
    tie = lax.optimization_barrier

    group = ("core",) + PLANE
    other = lax.ppermute(own, "zh", PAIR)
    lanes = split_lanes(own)
    near = lax.all_to_all(lanes.reshape(32, 2, 8, 8, 128), group, 0, 0, tiled=True)

    other, near, shard = tie((other, near, inverse_anc))
    sib = lax.ppermute(shard, "core", PAIR)
    lanes = split_lanes(other)
    far = lax.all_to_all(lanes.reshape(32, 2, 8, 8, 128), group, 0, 0, tiled=True)

    own = tie((own, lanes))[0]
    below = []
    for flip in (0, 8):
        moves = []
        for q in range(16):
            for h in range(2):
                for m in range(16):
                    moves.append((q * 32 + 16 * h + m, (m ^ flip) * 32 + 2 * q + h))
        below.append(lax.ppermute(own, ROW + COL, moves))
    below = jnp.stack(below)
    far, below = tie((far, below))

    near = near.reshape(2, 16, 2, 8, 8, 128)
    far = far.reshape(2, 16, 2, 8, 8, 128)
    parts = products(structure, ids, near, far, inverse_anc, sib)
    below, parts = tie((below, parts))
    below = doubled(below, "zb")
    got = lax.all_to_all(parts.astype(F16), ("zc", "h"), 0, 0, tiled=True).astype(F32)
    power = got[:, 1024:1025]
    most = jnp.max(power, axis=0, keepdims=True) + 2.0
    parts = jnp.sum(got[:, :1024] * jnp.exp2(power - most), axis=0).reshape(4, 256, 128)
    parts = jnp.concatenate([parts, jnp.broadcast_to(most, (4, 16, 128))], axis=1).astype(F16)

    below, parts = tie((below, parts))
    below = doubled(below, "zc")
    below = doubled(below, "core")
    got = lax.all_to_all(parts, ("za", "zb"), 0, 0, tiled=True).astype(F32)
    summed = jnp.sum(got[:, :256] * jnp.exp2(got[:, 256:257] - 14.0), axis=0)
    half, terms = diag_terms(ids, summed.reshape(2, 8, 16, 128), below)

    terms = lax.all_to_all(terms, PLANE, 0, 0, tiled=True)
    partner = lax.ppermute(half, "h", PAIR)
    part = jnp.sum(terms, axis=0)
    other, partner = tie((lax.ppermute(part, "zh", PAIR), partner))
    place = lax.axis_index(PLANE)
    start = lax.dynamic_index_in_dim(diag_inverse.reshape(16, 16, 256), place, 0, keepdims=False)
    diag = diag_copies(start, part, other)
    diag = lax.all_to_all(diag, PLANE, 0, 0, tiled=True)
    diag_block = diag.reshape(2, 8, 16, 256)

    first = my_col % 2 == 0
    left = jnp.where(first, half, partner)
    right = jnp.where(first, partner, half)
    block = jnp.concatenate([left, right], axis=-1)
    slots = lax.dynamic_index_in_dim(structure, my_col // 2, 1, keepdims=False)
    pieces = []
    for column in range(2):
        keep_it = (slots == 2 * my_col + column)[None, :, None, None]
        pieces.append(jnp.where(keep_it, block, jnp.zeros_like(block)))
    upper_inverse = jnp.concatenate(pieces, axis=3)
    return upper_inverse, diag_block


def solution(mesh):
    fine = Mesh(mesh.devices.reshape(2, 2, 2, 2, 2, 4, 2, 2), ROW + COL)
    placed = (
        P(None, ROW, COL),
        P(None, None, ROW, COL, None),
        P(None, None, ROW, None),
        P(),
    )
    return jax.shard_map(
        shards,
        mesh=fine,
        in_specs=placed,
        out_specs=(P(None, None, ROW, COL), P(None, None, ROW, None)),
        check_vma=False,
    )
```

```python
import jax
import jax.numpy as jnp
from jax import lax
from jax.experimental import pallas as pl
from jax.experimental.pallas import tpu as pltpu
from jax.sharding import Mesh, PartitionSpec as P

BF = jnp.bfloat16
F32 = jnp.float32
F16 = jnp.float16
ROW = ("za", "zb", "zc", "core")
COL = ("zh", "y", "xa", "h")
PLANE = ("y", "xa", "h")
VMEM_LIMIT = 48 * 1024 * 1024


def params():
    return pltpu.CompilerParams(vmem_limit_bytes=VMEM_LIMIT)


def whole(count):
    return [pl.BlockSpec(memory_space=pltpu.VMEM)] * count


def present(k, st, ids):
    return st[k, ids[1] // 2] // 2 == ids[1]


def block_at(k, row, st, ids):
    down = 256 * (st[k, row] - 4 * row)
    right = 256 * lax.rem(st[k, ids[1] // 2], 2)
    return down, right


def lanes_kernel(panel, out):
    x = panel[...].astype(F32).reshape(128, 256).astype(BF)
    src = lax.broadcasted_iota(jnp.int32, (256, 256), 0)
    dst = lax.broadcasted_iota(jnp.int32, (256, 256), 1)
    t = src % 16
    core = (src // 16) % 2
    zc = (src // 32) % 2
    zb = (src // 64) % 2
    za = src // 128
    place = core * 128 + zc * 64 + za * 32 + zb * 16 + t
    perm = jnp.where(place == dst, 1.0, 0.0).astype(BF)
    y = jnp.dot(x, perm, preferred_element_type=F32)
    for c in range(2):
        half = y[:, 128 * c : 128 * c + 128].reshape(2, 8, 8, 128).astype(BF)
        for z in range(16):
            out[c, z] = half


def split_lanes(panel):
    return pl.pallas_call(
        lanes_kernel,
        in_specs=whole(1),
        out_specs=whole(1)[0],
        out_shape=jax.ShapeDtypeStruct((2, 16, 2, 8, 8, 128), BF),
        compiler_params=params(),
    )(panel)


def product_kernel(st, ids, near, far, own, sib, out):
    core = ids[2]
    zh = ids[4]
    form = (((0,), (0,)), ((), ()))
    largest = jnp.zeros((8, 128), F32)
    for k in range(8):
        left, right_re, right_im = [], [], []
        for source, blocks in ((core, own), (1 - core, sib)):
            down, right = block_at(k, ids[0] - core + source, st, ids)
            for panel, half in ((near, zh), (far, 1 - zh)):
                rows = pl.ds(pl.multiple_of(down + 128 * half, 128), 128)
                lanes = pl.ds(pl.multiple_of(right, 256), 256)
                right_re.append(blocks[0, rows, lanes])
                right_im.append(blocks[1, rows, lanes])
                parts = [panel[source, :, p, k].reshape(128, 128) for p in range(2)]
                left.append(jnp.concatenate(parts, axis=1))
        left = jnp.concatenate(left, axis=0)
        right_re = jnp.concatenate(right_re, axis=0)
        right_im = jnp.concatenate(right_im, axis=0)
        one = lax.dot_general(left, right_re, form, preferred_element_type=F32)
        two = lax.dot_general(left, right_im, form, preferred_element_type=F32)
        total = jnp.concatenate([one[:128] - two[128:], one[128:] + two[:128]], axis=1)
        total = jnp.where(present(k, st, ids), total, 0.0)
        size = jnp.max(jnp.abs(total).reshape(16, 8, 512), axis=0)
        for lane in range(4):
            largest = jnp.maximum(largest, size[:, 128 * lane : 128 * lane + 128])
        for zc in range(2):
            for h in range(2):
                for zab in range(4):
                    for p in range(2):
                        row = 64 * zc + 16 * zab
                        lane = 256 * p + 128 * h
                        to = ((2 * zab + p) * 8 + k) * 16
                        out[2 * zc + h, to : to + 16] = total[row : row + 16, lane : lane + 128]
    largest = jnp.max(jnp.max(largest, axis=0, keepdims=True), axis=1, keepdims=True)
    power = jnp.clip(jnp.ceil(jnp.log2(largest)), -100.0, 100.0)
    scale = jnp.exp2(14.0 - power)
    for chunk in range(4):
        out[chunk, :1024] = out[chunk, :1024] * scale
        out[chunk, 1024:] = jnp.broadcast_to(power, (16, 128))


def products(structure, ids, near, far, own, sib):
    return pl.pallas_call(
        product_kernel,
        in_specs=[pl.BlockSpec(memory_space=pltpu.SMEM)] * 2 + whole(4),
        out_specs=whole(1)[0],
        out_shape=jax.ShapeDtypeStruct((4, 1040, 128), F32),
        compiler_params=params(),
    )(structure, ids, near, far, own, sib)


def diag_kernel(ids, summed, below, half, out):
    row = ids[0]
    for k in range(8):
        left = []
        for p in range(2):
            upper = (-summed[p, k]).astype(BF)
            half[p, k] = upper
            left.append(upper)
        left = jnp.concatenate(left, axis=0)
        panel = []
        for p in range(2):
            part = []
            for m in range(16):
                far = jnp.bitwise_xor(row, m)
                at = (far % 2) * 8 + (far // 2 % 2) * 4 + (far // 4 % 2) * 2 + far // 8
                part.append(below[at, p, k].astype(F32))
            panel.append(jnp.concatenate(part, axis=0).astype(BF))
        one = jnp.dot(left, panel[0], preferred_element_type=F32)
        two = jnp.dot(left, panel[1], preferred_element_type=F32)
        out[k] = one[:16] - two[16:]
        out[8 + k] = two[:16] + one[16:]


def diag_terms(ids, summed, below):
    return pl.pallas_call(
        diag_kernel,
        in_specs=[pl.BlockSpec(memory_space=pltpu.SMEM)] + whole(2),
        out_specs=whole(2),
        out_shape=[
            jax.ShapeDtypeStruct((2, 8, 16, 128), BF),
            jax.ShapeDtypeStruct((16, 16, 256), F32),
        ],
        compiler_params=params(),
    )(ids, summed, below)


def copies_kernel(start, part, other, out):
    value = start[...] - (part[...] + other[...])
    for chip in range(16):
        out[chip] = value


def diag_copies(start, part, other):
    return pl.pallas_call(
        copies_kernel,
        in_specs=whole(3),
        out_specs=whole(1)[0],
        out_shape=jax.ShapeDtypeStruct((16, 16, 256), F32),
        compiler_params=params(),
    )(start, part, other)


PAIR = [(0, 1), (1, 0)]


def doubled(value, axis):
    return jnp.concatenate([value, lax.ppermute(value, axis, PAIR)], axis=0)


def shards(inverse_anc, lower_panel, diag_inverse, structure):
    my_row = lax.axis_index(ROW)
    my_col = lax.axis_index(COL)
    ids = [my_row, my_col] + [lax.axis_index(axis) for axis in ("core", "zc", "zh", "zb", "za")]
    ids = jnp.stack(ids).astype(jnp.int32)
    own = lower_panel.reshape(2, 8, 8, 256)
    tie = lax.optimization_barrier

    group = ("core",) + PLANE
    other = lax.ppermute(own, "zh", PAIR)
    lanes = split_lanes(own)
    near = lax.all_to_all(lanes.reshape(32, 2, 8, 8, 128), group, 0, 0, tiled=True)

    other, near, shard = tie((other, near, inverse_anc))
    sib = lax.ppermute(shard, "core", PAIR)
    lanes = split_lanes(other)
    far = lax.all_to_all(lanes.reshape(32, 2, 8, 8, 128), group, 0, 0, tiled=True)

    own = tie((own, lanes))[0]
    below = []
    for flip in (0, 8):
        moves = []
        for q in range(16):
            for h in range(2):
                for m in range(16):
                    moves.append((q * 32 + 16 * h + m, (m ^ flip) * 32 + 2 * q + h))
        below.append(lax.ppermute(own, ROW + COL, moves))
    below = jnp.stack(below)

    near = near.reshape(2, 16, 2, 8, 8, 128)
    far = far.reshape(2, 16, 2, 8, 8, 128)
    parts = products(structure, ids, near, far, inverse_anc, sib)
    below, parts = tie((below, parts))
    below = doubled(below, "zb")
    got = lax.all_to_all(parts.astype(F16), ("zc", "h"), 0, 0, tiled=True).astype(F32)
    power = got[:, 1024:1025]
    most = jnp.max(power, axis=0, keepdims=True) + 2.0
    parts = jnp.sum(got[:, :1024] * jnp.exp2(power - most), axis=0).reshape(4, 256, 128)
    parts = jnp.concatenate([parts, jnp.broadcast_to(most, (4, 16, 128))], axis=1).astype(F16)

    below, parts = tie((below, parts))
    below = doubled(below, "zc")
    below = doubled(below, "core")
    got = lax.all_to_all(parts, ("za", "zb"), 0, 0, tiled=True).astype(F32)
    summed = jnp.sum(got[:, :256] * jnp.exp2(got[:, 256:257] - 14.0), axis=0)
    half, terms = diag_terms(ids, summed.reshape(2, 8, 16, 128), below)

    terms = lax.all_to_all(terms, PLANE, 0, 0, tiled=True)
    partner = lax.ppermute(half, "h", PAIR)
    part = jnp.sum(terms, axis=0)
    other, partner = tie((lax.ppermute(part, "zh", PAIR), partner))
    place = lax.axis_index(PLANE)
    start = lax.dynamic_index_in_dim(diag_inverse.reshape(16, 16, 256), place, 0, keepdims=False)
    diag = diag_copies(start, part, other)
    diag = lax.all_to_all(diag, PLANE, 0, 0, tiled=True)
    diag_block = diag.reshape(2, 8, 16, 256)

    first = my_col % 2 == 0
    left = jnp.where(first, half, partner)
    right = jnp.where(first, partner, half)
    block = jnp.concatenate([left, right], axis=-1)
    slots = lax.dynamic_index_in_dim(structure, my_col // 2, 1, keepdims=False)
    pieces = []
    for column in range(2):
        keep_it = (slots == 2 * my_col + column)[None, :, None, None]
        pieces.append(jnp.where(keep_it, block, jnp.zeros_like(block)))
    upper_inverse = jnp.concatenate(pieces, axis=3)
    return upper_inverse, diag_block


def solution(mesh):
    fine = Mesh(mesh.devices.reshape(2, 2, 2, 2, 2, 4, 2, 2), ROW + COL)
    placed = (
        P(None, ROW, COL),
        P(None, None, ROW, COL, None),
        P(None, None, ROW, None),
        P(),
    )
    return jax.shard_map(
        shards,
        mesh=fine,
        in_specs=placed,
        out_specs=(P(None, None, ROW, COL), P(None, None, ROW, None)),
        check_vma=False,
    )
```

```python
import jax
import jax.numpy as jnp
from jax import lax
from jax.experimental import pallas as pl
from jax.experimental.pallas import tpu as pltpu
from jax.sharding import Mesh, PartitionSpec as P

BF = jnp.bfloat16
F32 = jnp.float32
F16 = jnp.float16
ROW = ("za", "zb", "zc", "core")
COL = ("zh", "y", "xa", "h")
PLANE = ("y", "xa", "h")
VMEM_LIMIT = 48 * 1024 * 1024


def params():
    return pltpu.CompilerParams(vmem_limit_bytes=VMEM_LIMIT)


def whole(count):
    return [pl.BlockSpec(memory_space=pltpu.VMEM)] * count


def present(k, st, ids):
    return st[k, ids[1] // 2] // 2 == ids[1]


def block_at(k, row, st, ids):
    down = 256 * (st[k, row] - 4 * row)
    right = 256 * lax.rem(st[k, ids[1] // 2], 2)
    return down, right


def lanes_kernel(panel, out):
    x = panel[...].astype(F32).reshape(128, 256).astype(BF)
    src = lax.broadcasted_iota(jnp.int32, (256, 256), 0)
    dst = lax.broadcasted_iota(jnp.int32, (256, 256), 1)
    t = src % 16
    core = (src // 16) % 2
    zc = (src // 32) % 2
    zb = (src // 64) % 2
    za = src // 128
    place = core * 128 + zc * 64 + za * 32 + zb * 16 + t
    perm = jnp.where(place == dst, 1.0, 0.0).astype(BF)
    y = jnp.dot(x, perm, preferred_element_type=F32)
    for c in range(2):
        half = y[:, 128 * c : 128 * c + 128].reshape(2, 8, 8, 128).astype(BF)
        for z in range(16):
            out[c, z] = half


def split_lanes(panel):
    return pl.pallas_call(
        lanes_kernel,
        in_specs=whole(1),
        out_specs=whole(1)[0],
        out_shape=jax.ShapeDtypeStruct((2, 16, 2, 8, 8, 128), BF),
        compiler_params=params(),
    )(panel)


def product_kernel(st, ids, near, far, own, sib, out):
    core = ids[2]
    zh = ids[4]
    form = (((0,), (0,)), ((), ()))
    largest = jnp.zeros((8, 128), F32)
    for k in range(8):
        left, right_re, right_im = [], [], []
        for source, blocks in ((core, own), (1 - core, sib)):
            down, right = block_at(k, ids[0] - core + source, st, ids)
            for panel, half in ((near, zh), (far, 1 - zh)):
                rows = pl.ds(pl.multiple_of(down + 128 * half, 128), 128)
                lanes = pl.ds(pl.multiple_of(right, 256), 256)
                right_re.append(blocks[0, rows, lanes])
                right_im.append(blocks[1, rows, lanes])
                parts = [panel[source, :, p, k].reshape(128, 128) for p in range(2)]
                left.append(jnp.concatenate(parts, axis=1))
        left = jnp.concatenate(left, axis=0)
        right_re = jnp.concatenate(right_re, axis=0)
        right_im = jnp.concatenate(right_im, axis=0)
        one = lax.dot_general(left, right_re, form, preferred_element_type=F32)
        two = lax.dot_general(left, right_im, form, preferred_element_type=F32)
        total = jnp.concatenate([one[:128] - two[128:], one[128:] + two[:128]], axis=1)
        total = jnp.where(present(k, st, ids), total, 0.0)
        size = jnp.max(jnp.abs(total).reshape(16, 8, 512), axis=0)
        for lane in range(4):
            largest = jnp.maximum(largest, size[:, 128 * lane : 128 * lane + 128])
        for zc in range(2):
            for h in range(2):
                for zab in range(4):
                    for p in range(2):
                        row = 64 * zc + 16 * zab
                        lane = 256 * p + 128 * h
                        to = ((2 * zab + p) * 8 + k) * 16
                        out[2 * zc + h, to : to + 16] = total[row : row + 16, lane : lane + 128]
    largest = jnp.max(jnp.max(largest, axis=0, keepdims=True), axis=1, keepdims=True)
    power = jnp.clip(jnp.ceil(jnp.log2(largest)), -100.0, 100.0)
    scale = jnp.exp2(14.0 - power)
    for chunk in range(4):
        out[chunk, :1024] = out[chunk, :1024] * scale
        out[chunk, 1024:] = jnp.broadcast_to(power, (16, 128))


def products(structure, ids, near, far, own, sib):
    return pl.pallas_call(
        product_kernel,
        in_specs=[pl.BlockSpec(memory_space=pltpu.SMEM)] * 2 + whole(4),
        out_specs=whole(1)[0],
        out_shape=jax.ShapeDtypeStruct((4, 1040, 128), F32),
        compiler_params=params(),
    )(structure, ids, near, far, own, sib)


def diag_kernel(ids, summed, below, half, out):
    row = ids[0]
    for k in range(8):
        left = []
        for p in range(2):
            upper = (-summed[p, k]).astype(BF)
            half[p, k] = upper
            left.append(upper)
        left = jnp.concatenate(left, axis=0)
        panel = []
        for p in range(2):
            part = []
            for m in range(16):
                far = jnp.bitwise_xor(row, m)
                at = (far % 2) * 8 + (far // 2 % 2) * 4 + (far // 4 % 2) * 2 + far // 8
                part.append(below[at, p, k].astype(F32))
            panel.append(jnp.concatenate(part, axis=0).astype(BF))
        one = jnp.dot(left, panel[0], preferred_element_type=F32)
        two = jnp.dot(left, panel[1], preferred_element_type=F32)
        out[k] = one[:16] - two[16:]
        out[8 + k] = two[:16] + one[16:]


def diag_terms(ids, summed, below):
    return pl.pallas_call(
        diag_kernel,
        in_specs=[pl.BlockSpec(memory_space=pltpu.SMEM)] + whole(2),
        out_specs=whole(2),
        out_shape=[
            jax.ShapeDtypeStruct((2, 8, 16, 128), BF),
            jax.ShapeDtypeStruct((16, 16, 256), F32),
        ],
        compiler_params=params(),
    )(ids, summed, below)


def copies_kernel(start, part, other, out):
    value = start[...] - (part[...] + other[...])
    for chip in range(16):
        out[chip] = value


def diag_copies(start, part, other):
    return pl.pallas_call(
        copies_kernel,
        in_specs=whole(3),
        out_specs=whole(1)[0],
        out_shape=jax.ShapeDtypeStruct((16, 16, 256), F32),
        compiler_params=params(),
    )(start, part, other)


PAIR = [(0, 1), (1, 0)]


def doubled(value, axis):
    return jnp.concatenate([value, lax.ppermute(value, axis, PAIR)], axis=0)


def shards(inverse_anc, lower_panel, diag_inverse, structure):
    my_row = lax.axis_index(ROW)
    my_col = lax.axis_index(COL)
    ids = [my_row, my_col] + [lax.axis_index(axis) for axis in ("core", "zc", "zh", "zb", "za")]
    ids = jnp.stack(ids).astype(jnp.int32)
    own = lower_panel.reshape(2, 8, 8, 256)
    tie = lax.optimization_barrier

    group = ("core",) + PLANE
    other = lax.ppermute(own, "zh", PAIR)
    lanes = split_lanes(own)
    near = lax.all_to_all(lanes.reshape(32, 2, 8, 8, 128), group, 0, 0, tiled=True)

    other, near, shard = tie((other, near, inverse_anc))
    sib = lax.ppermute(shard, "core", PAIR)
    lanes = split_lanes(other)
    far = lax.all_to_all(lanes.reshape(32, 2, 8, 8, 128), group, 0, 0, tiled=True)

    own = tie((own, lanes))[0]
    below = []
    for flip in (0, 8):
        moves = []
        for q in range(16):
            for h in range(2):
                for m in range(16):
                    moves.append((q * 32 + 16 * h + m, (m ^ flip) * 32 + 2 * q + h))
        below.append(lax.ppermute(own, ROW + COL, moves))
    below = jnp.stack(below)

    near = near.reshape(2, 16, 2, 8, 8, 128)
    far = far.reshape(2, 16, 2, 8, 8, 128)
    parts = products(structure, ids, near, far, inverse_anc, sib)
    below, parts = tie((below, parts))
    below = doubled(below, "zb")
    got = lax.all_to_all(parts.astype(F16), ("zc", "h"), 0, 0, tiled=True).astype(F32)
    power = got[:, 1024:1025]
    most = jnp.max(power, axis=0, keepdims=True) + 2.0
    parts = jnp.sum(got[:, :1024] * jnp.exp2(power - most), axis=0).reshape(4, 256, 128)
    parts = jnp.concatenate([parts, jnp.broadcast_to(most, (4, 16, 128))], axis=1).astype(F16)

    below = doubled(below, "zc")
    below = doubled(below, "core")
    got = lax.all_to_all(parts, ("za", "zb"), 0, 0, tiled=True).astype(F32)
    summed = jnp.sum(got[:, :256] * jnp.exp2(got[:, 256:257] - 14.0), axis=0)
    half, terms = diag_terms(ids, summed.reshape(2, 8, 16, 128), below)

    terms = lax.all_to_all(terms, PLANE, 0, 0, tiled=True)
    partner = lax.ppermute(half, "h", PAIR)
    part = jnp.sum(terms, axis=0)
    other, partner = tie((lax.ppermute(part, "zh", PAIR), partner))
    place = lax.axis_index(PLANE)
    start = lax.dynamic_index_in_dim(diag_inverse.reshape(16, 16, 256), place, 0, keepdims=False)
    diag = diag_copies(start, part, other)
    diag = lax.all_to_all(diag, PLANE, 0, 0, tiled=True)
    diag_block = diag.reshape(2, 8, 16, 256)

    first = my_col % 2 == 0
    left = jnp.where(first, half, partner)
    right = jnp.where(first, partner, half)
    block = jnp.concatenate([left, right], axis=-1)
    slots = lax.dynamic_index_in_dim(structure, my_col // 2, 1, keepdims=False)
    pieces = []
    for column in range(2):
        keep_it = (slots == 2 * my_col + column)[None, :, None, None]
        pieces.append(jnp.where(keep_it, block, jnp.zeros_like(block)))
    upper_inverse = jnp.concatenate(pieces, axis=3)
    return upper_inverse, diag_block


def solution(mesh):
    fine = Mesh(mesh.devices.reshape(2, 2, 2, 2, 2, 4, 2, 2), ROW + COL)
    placed = (
        P(None, ROW, COL),
        P(None, None, ROW, COL, None),
        P(None, None, ROW, None),
        P(),
    )
    return jax.shard_map(
        shards,
        mesh=fine,
        in_specs=placed,
        out_specs=(P(None, None, ROW, COL), P(None, None, ROW, None)),
        check_vma=False,
    )
```

```python
import jax
import jax.numpy as jnp
from jax import lax
from jax.experimental import pallas as pl
from jax.experimental.pallas import tpu as pltpu
from jax.sharding import Mesh, PartitionSpec as P

BF = jnp.bfloat16
F32 = jnp.float32
F16 = jnp.float16
ROW = ("za", "zb", "zc", "core")
COL = ("zh", "y", "xa", "h")
PLANE = ("y", "xa", "h")
VMEM_LIMIT = 48 * 1024 * 1024


def params():
    return pltpu.CompilerParams(vmem_limit_bytes=VMEM_LIMIT)


def whole(count):
    return [pl.BlockSpec(memory_space=pltpu.VMEM)] * count


def present(k, st, ids):
    return st[k, ids[1] // 2] // 2 == ids[1]


def block_at(k, row, st, ids):
    down = 256 * (st[k, row] - 4 * row)
    right = 256 * lax.rem(st[k, ids[1] // 2], 2)
    return down, right


def lanes_kernel(panel, out):
    x = panel[...].astype(F32).reshape(128, 256).astype(BF)
    src = lax.broadcasted_iota(jnp.int32, (256, 256), 0)
    dst = lax.broadcasted_iota(jnp.int32, (256, 256), 1)
    t = src % 16
    core = (src // 16) % 2
    zc = (src // 32) % 2
    zb = (src // 64) % 2
    za = src // 128
    place = core * 128 + zc * 64 + za * 32 + zb * 16 + t
    perm = jnp.where(place == dst, 1.0, 0.0).astype(BF)
    y = jnp.dot(x, perm, preferred_element_type=F32)
    for c in range(2):
        half = y[:, 128 * c : 128 * c + 128].reshape(2, 8, 8, 128).astype(BF)
        for z in range(16):
            out[c, z] = half


def split_lanes(panel):
    return pl.pallas_call(
        lanes_kernel,
        in_specs=whole(1),
        out_specs=whole(1)[0],
        out_shape=jax.ShapeDtypeStruct((2, 16, 2, 8, 8, 128), BF),
        compiler_params=params(),
    )(panel)


def product_kernel(st, ids, near, far, own, sib, out):
    core = ids[2]
    zh = ids[4]
    form = (((0,), (0,)), ((), ()))
    largest = jnp.zeros((8, 128), F32)
    for k in range(8):
        left, right_re, right_im = [], [], []
        for source, blocks in ((core, own), (1 - core, sib)):
            down, right = block_at(k, ids[0] - core + source, st, ids)
            for panel, half in ((near, zh), (far, 1 - zh)):
                rows = pl.ds(pl.multiple_of(down + 128 * half, 128), 128)
                lanes = pl.ds(pl.multiple_of(right, 256), 256)
                right_re.append(blocks[0, rows, lanes])
                right_im.append(blocks[1, rows, lanes])
                parts = [panel[source, :, p, k].reshape(128, 128) for p in range(2)]
                left.append(jnp.concatenate(parts, axis=1))
        left = jnp.concatenate(left, axis=0)
        right_re = jnp.concatenate(right_re, axis=0)
        right_im = jnp.concatenate(right_im, axis=0)
        one = lax.dot_general(left, right_re, form, preferred_element_type=F32)
        two = lax.dot_general(left, right_im, form, preferred_element_type=F32)
        total = jnp.concatenate([one[:128] - two[128:], one[128:] + two[:128]], axis=1)
        total = jnp.where(present(k, st, ids), total, 0.0)
        size = jnp.max(jnp.abs(total).reshape(16, 8, 512), axis=0)
        for lane in range(4):
            largest = jnp.maximum(largest, size[:, 128 * lane : 128 * lane + 128])
        for zc in range(2):
            for h in range(2):
                for zab in range(4):
                    for p in range(2):
                        row = 64 * zc + 16 * zab
                        lane = 256 * p + 128 * h
                        to = ((2 * zab + p) * 8 + k) * 16
                        out[2 * zc + h, to : to + 16] = total[row : row + 16, lane : lane + 128]
    largest = jnp.max(jnp.max(largest, axis=0, keepdims=True), axis=1, keepdims=True)
    power = jnp.clip(jnp.ceil(jnp.log2(largest)), -100.0, 100.0)
    scale = jnp.exp2(14.0 - power)
    for chunk in range(4):
        out[chunk, :1024] = out[chunk, :1024] * scale
        out[chunk, 1024:] = jnp.broadcast_to(power, (16, 128))


def products(structure, ids, near, far, own, sib):
    return pl.pallas_call(
        product_kernel,
        in_specs=[pl.BlockSpec(memory_space=pltpu.SMEM)] * 2 + whole(4),
        out_specs=whole(1)[0],
        out_shape=jax.ShapeDtypeStruct((4, 1040, 128), F32),
        compiler_params=params(),
    )(structure, ids, near, far, own, sib)


def diag_kernel(ids, summed, below, half, out):
    row = ids[0]
    for k in range(8):
        left = []
        for p in range(2):
            upper = (-summed[p, k]).astype(BF)
            half[p, k] = upper
            left.append(upper)
        left = jnp.concatenate(left, axis=0)
        panel = []
        for p in range(2):
            part = []
            for m in range(16):
                far = jnp.bitwise_xor(row, m)
                at = (far % 2) * 8 + (far // 2 % 2) * 4 + (far // 4 % 2) * 2 + far // 8
                part.append(below[at, p, k].astype(F32))
            panel.append(jnp.concatenate(part, axis=0).astype(BF))
        one = jnp.dot(left, panel[0], preferred_element_type=F32)
        two = jnp.dot(left, panel[1], preferred_element_type=F32)
        out[k] = one[:16] - two[16:]
        out[8 + k] = two[:16] + one[16:]


def diag_terms(ids, summed, below):
    return pl.pallas_call(
        diag_kernel,
        in_specs=[pl.BlockSpec(memory_space=pltpu.SMEM)] + whole(2),
        out_specs=whole(2),
        out_shape=[
            jax.ShapeDtypeStruct((2, 8, 16, 128), BF),
            jax.ShapeDtypeStruct((16, 16, 256), F32),
        ],
        compiler_params=params(),
    )(ids, summed, below)


def copies_kernel(start, part, other, out):
    value = start[...] - (part[...] + other[...])
    for chip in range(16):
        out[chip] = value


def diag_copies(start, part, other):
    return pl.pallas_call(
        copies_kernel,
        in_specs=whole(3),
        out_specs=whole(1)[0],
        out_shape=jax.ShapeDtypeStruct((16, 16, 256), F32),
        compiler_params=params(),
    )(start, part, other)


PAIR = [(0, 1), (1, 0)]


def doubled(value, axis):
    return jnp.concatenate([value, lax.ppermute(value, axis, PAIR)], axis=0)


def shards(inverse_anc, lower_panel, diag_inverse, structure):
    my_row = lax.axis_index(ROW)
    my_col = lax.axis_index(COL)
    ids = [my_row, my_col] + [lax.axis_index(axis) for axis in ("core", "zc", "zh", "zb", "za")]
    ids = jnp.stack(ids).astype(jnp.int32)
    own = lower_panel.reshape(2, 8, 8, 256)
    tie = lax.optimization_barrier

    group = ("core",) + PLANE
    other = lax.ppermute(own, "zh", PAIR)
    lanes = split_lanes(own)
    near = lax.all_to_all(lanes.reshape(32, 2, 8, 8, 128), group, 0, 0, tiled=True)

    other, near, shard = tie((other, near, inverse_anc))
    sib = lax.ppermute(shard, "core", PAIR)
    lanes = split_lanes(other)
    far = lax.all_to_all(lanes.reshape(32, 2, 8, 8, 128), group, 0, 0, tiled=True)

    own = tie((own, lanes))[0]
    below = []
    for flip in (0, 8):
        moves = []
        for q in range(16):
            for h in range(2):
                for m in range(16):
                    moves.append((q * 32 + 16 * h + m, (m ^ flip) * 32 + 2 * q + h))
        below.append(lax.ppermute(own, ROW + COL, moves))
    below = jnp.stack(below)

    near = near.reshape(2, 16, 2, 8, 8, 128)
    far = far.reshape(2, 16, 2, 8, 8, 128)
    parts = products(structure, ids, near, far, inverse_anc, sib)
    below = doubled(below, "zb")
    got = lax.all_to_all(parts.astype(F16), ("zc", "h"), 0, 0, tiled=True).astype(F32)
    power = got[:, 1024:1025]
    most = jnp.max(power, axis=0, keepdims=True) + 2.0
    parts = jnp.sum(got[:, :1024] * jnp.exp2(power - most), axis=0).reshape(4, 256, 128)
    parts = jnp.concatenate([parts, jnp.broadcast_to(most, (4, 16, 128))], axis=1).astype(F16)

    below = doubled(below, "zc")
    below = doubled(below, "core")
    got = lax.all_to_all(parts, ("za", "zb"), 0, 0, tiled=True).astype(F32)
    summed = jnp.sum(got[:, :256] * jnp.exp2(got[:, 256:257] - 14.0), axis=0)
    half, terms = diag_terms(ids, summed.reshape(2, 8, 16, 128), below)

    terms = lax.all_to_all(terms, PLANE, 0, 0, tiled=True)
    partner = lax.ppermute(half, "h", PAIR)
    part = jnp.sum(terms, axis=0)
    other, partner = tie((lax.ppermute(part, "zh", PAIR), partner))
    place = lax.axis_index(PLANE)
    start = lax.dynamic_index_in_dim(diag_inverse.reshape(16, 16, 256), place, 0, keepdims=False)
    diag = diag_copies(start, part, other)
    diag = lax.all_to_all(diag, PLANE, 0, 0, tiled=True)
    diag_block = diag.reshape(2, 8, 16, 256)

    first = my_col % 2 == 0
    left = jnp.where(first, half, partner)
    right = jnp.where(first, partner, half)
    block = jnp.concatenate([left, right], axis=-1)
    slots = lax.dynamic_index_in_dim(structure, my_col // 2, 1, keepdims=False)
    pieces = []
    for column in range(2):
        keep_it = (slots == 2 * my_col + column)[None, :, None, None]
        pieces.append(jnp.where(keep_it, block, jnp.zeros_like(block)))
    upper_inverse = jnp.concatenate(pieces, axis=3)
    return upper_inverse, diag_block


def solution(mesh):
    fine = Mesh(mesh.devices.reshape(2, 2, 2, 2, 2, 4, 2, 2), ROW + COL)
    placed = (
        P(None, ROW, COL),
        P(None, None, ROW, COL, None),
        P(None, None, ROW, None),
        P(),
    )
    return jax.shard_map(
        shards,
        mesh=fine,
        in_specs=placed,
        out_specs=(P(None, None, ROW, COL), P(None, None, ROW, None)),
        check_vma=False,
    )
```
